32 devices in a mesh: gx: 4 (over x, core), gy: 2 (over y), gz: 4 (over z).
Axes of the slice: x: 2, y: 2, z: 4, core: 2. Of those that a mesh axis runs over, the one named last changes fastest.
Arguments:
- cotangent: float32 [16, 128, 512], P('gx', 'gy', 'gz'), may hold values from -6 to 6
- fraction_x: float32 [16, 128, 512], P('gx', 'gy', 'gz'), may hold values from 0 to 1
- fraction_y: float32 [16, 128, 512], P('gx', 'gy', 'gz'), may hold values from 0 to 1
- fraction_z: float32 [16, 128, 512], P('gx', 'gy', 'gz'), may hold values from 0 to 1
- courant_x: float32 [16, 128, 512], P('gx', 'gy', 'gz'), may hold values from -0.3 to 0.3
- courant_y: float32 [16, 128, 512], P('gx', 'gy', 'gz'), may hold values from -0.3 to 0.3
- courant_z: float32 [16, 128, 512], P('gx', 'gy', 'gz'), may hold values from -0.3 to 0.3
- open_cells: int32 [16, 128, 512], P('gx', 'gy', 'gz'), may hold values 0 or 1
Outputs:
- adjoint_fraction: float32 [16, 128, 512], P('gx', 'gy', 'gz')
The draws below stay inside these ranges and needn't reach their ends.
All inputs are finite; a program needn't handle non-finite values. No bound on the sum of `open_cells` on one device may be relied on, other than what follows from the above.
Results may differ from the reference program's by a relative error of at most 0.0003.
Values sent between devices are 32-bit elements; how exact they have to be, the bound alone decides.
No kernel may reach another device: no remote copies, remote signals or barrier semaphores. Data moves between devices by JAX's collectives and lax.ppermute only.
A program may use at most 64 MiB of HBM per device.

```python
import jax
import jax.numpy as jnp
from jax import lax

NX = 16
NY = 128
NZ = 512


def touch_ends(drawn, key, smallest, high):
    longest = drawn.shape.index(max(drawn.shape))
    spots = []
    for shift in (0, 1):
        where = [jax.random.randint(jax.random.fold_in(key, axis), (), 0, length) for axis, length in enumerate(drawn.shape)]
        where[longest] = (where[longest] + shift) % drawn.shape[longest]
        spots.append(tuple(where))
    return drawn.at[spots[0]].set(smallest).at[spots[1]].set(high)


def block_levels(stream_key, shape, pieces, smallest, largest):
    level = 1.0
    for axis_at, blocks in pieces:
        steps = jax.random.uniform(jax.random.fold_in(jax.random.fold_in(stream_key, 6), axis_at), (blocks,), jnp.float32, smallest / len(pieces), largest / len(pieces))
        level = level * jnp.repeat(jnp.exp(steps), shape[axis_at] // blocks).reshape((-1,) + (1,) * (len(shape) - 1 - axis_at))
    return level


def normal_values(stream_key, extent, deviation, bound, split=(), dtype=jnp.bfloat16):
    array = deviation * jax.random.normal(stream_key, extent, jnp.float32)
    if split:
        array = array * block_levels(stream_key, extent, split, -0.22, 0.18)
    return jnp.clip(array, -bound, bound).astype(dtype)


def setup_inputs(seed: int = 0) -> dict:
    splits = jax.random.split(jax.random.key(seed), 9)
    cotangent = normal_values(splits[0], (NX, NY, NZ), 1.0, 6.0, ((0, 4), (1, 2), (2, 4)), jnp.float32)
    fraction_x = jnp.clip(1.0 * jax.random.uniform(splits[1], (NX, NY, NZ), jnp.float32) ** block_levels(splits[1], (NX, NY, NZ), ((0, 4), (1, 2), (2, 4)), -0.2, 0.2), 0.0, 1.0)
    fraction_y = jnp.clip(1.0 * jax.random.uniform(splits[2], (NX, NY, NZ), jnp.float32) ** block_levels(splits[2], (NX, NY, NZ), ((0, 4), (1, 2), (2, 4)), -0.2, 0.2), 0.0, 1.0)
    fraction_z = jnp.clip(1.0 * jax.random.uniform(splits[3], (NX, NY, NZ), jnp.float32) ** block_levels(splits[3], (NX, NY, NZ), ((0, 4), (1, 2), (2, 4)), -0.2, 0.2), 0.0, 1.0)
    courant_x = jnp.clip(jax.random.uniform(splits[4], (NX, NY, NZ), jnp.float32, -0.3, 0.3) * block_levels(splits[4], (NX, NY, NZ), ((0, 4), (1, 2), (2, 4)), -0.4, 0.0), -0.3, 0.3)
    courant_y = jnp.clip(jax.random.uniform(splits[5], (NX, NY, NZ), jnp.float32, -0.3, 0.3) * block_levels(splits[5], (NX, NY, NZ), ((0, 4), (1, 2), (2, 4)), -0.4, 0.0), -0.3, 0.3)
    courant_z = jnp.clip(jax.random.uniform(splits[6], (NX, NY, NZ), jnp.float32, -0.3, 0.3) * block_levels(splits[6], (NX, NY, NZ), ((0, 4), (1, 2), (2, 4)), -0.4, 0.0), -0.3, 0.3)
    open_cells = touch_ends((jax.random.randint(splits[7], (NX, NY, NZ), 0, 10) < 9).astype(jnp.int32), jax.random.fold_in(splits[7], 1), 0, 1)
    return dict(cotangent=cotangent, fraction_x=fraction_x, fraction_y=fraction_y, fraction_z=fraction_z, courant_x=courant_x, courant_y=courant_y, courant_z=courant_z, open_cells=open_cells)


sharpness = 3.5

def face_flux(padded, face_rates, along, count):
    before = lax.slice_in_dim(padded, 0, count + 1, axis=along)
    current = lax.slice_in_dim(padded, 1, count + 2, axis=along)
    after = lax.slice_in_dim(padded, 2, count + 3, axis=along)
    further = lax.slice_in_dim(padded, 3, count + 4, axis=along)
    forward = face_rates >= 0.0
    upwind = jnp.where(forward, current, after)
    behind = jnp.where(forward, before, further)
    ahead = jnp.where(forward, after, current)
    slope = jnp.tanh(sharpness * (ahead - behind))
    return face_rates * (upwind + 0.5 * upwind * (1.0 - upwind) * slope)

def change(padded, face_rates, along):
    count = padded.shape[along] - 4
    flux = face_flux(padded, face_rates, along, count)
    lower = lax.slice_in_dim(flux, 0, count, axis=along)
    upper = lax.slice_in_dim(flux, 1, count + 1, axis=along)
    cells = lax.slice_in_dim(padded, 2, count + 2, axis=along)
    rate_lower = lax.slice_in_dim(face_rates, 0, count, axis=along)
    rate_upper = lax.slice_in_dim(face_rates, 1, count + 1, axis=along)
    return lower - upper + cells * (rate_upper - rate_lower)

def sweep_adjoint(fraction, courant, opened, adjoint, along):
    count = fraction.shape[along]
    cell_pad = [(0, 0), (0, 0), (0, 0)]
    cell_pad[along] = (2, 2)
    face_pad = [(0, 0), (0, 0), (0, 0)]
    face_pad[along] = (1, 0)
    padded = jnp.pad(fraction, cell_pad)
    face_rates = jnp.pad(courant, face_pad)
    _, pullback = jax.vjp(lambda cells: change(cells, face_rates, along), padded)
    pulled = pullback(opened * adjoint)[0]
    return adjoint + lax.slice_in_dim(pulled, 2, count + 2, axis=along)

def reference(cotangent, fraction_x, fraction_y, fraction_z, courant_x, courant_y, courant_z, open_cells):
    opened = open_cells.astype(jnp.float32)
    adjoint = sweep_adjoint(fraction_z, courant_z, opened, cotangent, 2)
    adjoint = sweep_adjoint(fraction_y, courant_y, opened, adjoint, 1)
    adjoint = sweep_adjoint(fraction_x, courant_x, opened, adjoint, 0)
    return adjoint
```

```python
import functools

import jax
import jax.numpy as jnp
from jax import lax
from jax.experimental import pallas as pl
from jax.experimental.pallas import tpu as pltpu
from jax.sharding import PartitionSpec as P

sharpness = 3.5
slot = 8
AXES = ("gx", "gy", "gz")


def pair_rounds(sizes, along):
    size = sizes[along]
    if size == 1:
        return []
    assert size % 2 == 0

    def perm(partner):
        pairs = []
        for i in range(sizes[0]):
            for j in range(sizes[1]):
                for k in range(sizes[2]):
                    a, b, c = partner(i, j, k)
                    pairs.append(
                        ((i * sizes[1] + j) * sizes[2] + k, (a * sizes[1] + b) * sizes[2] + c)
                    )
        return pairs

    def even(*at):
        at = list(at)
        at[along] ^= 1
        return at

    def odd(*at):
        at = list(at)
        if 0 < at[along] < size - 1:
            at[along] = (at[along] - 1) ^ 1
            at[along] += 1
        elif along != 0 and sizes[0] % 2 == 0:
            at[0] ^= 1
        else:
            at[along] = size - 1 - at[along]
        return at

    return [perm(even)] if size == 2 else [perm(even), perm(odd)]


def roles(axis, size):
    at = lax.axis_index(axis)
    return lax.rem(at, 2) == 0, at > 0, at < size - 1


def to_send(axis, size, up, down):
    if size == 1:
        return []
    even, _, _ = roles(axis, size)
    first = jnp.where(even, up, down)
    return [first] if size == 2 else [first, jnp.where(even, down, up)]


def received(axis, size, messages, like):
    if size == 1:
        return jnp.zeros_like(like), jnp.zeros_like(like)
    even, has_low, has_high = roles(axis, size)
    first, second = messages[0], messages[-1]
    low = jnp.where(even, second, first)
    high = jnp.where(even, first, second)
    return jnp.where(has_low, low, 0.0), jnp.where(has_high, high, 0.0)


def bend(a, difference):
    t = jnp.tanh(sharpness * difference)
    return t, 0.5 * sharpness * a * (1.0 - a) * (1.0 - t * t)


def lower_carry(w, c, a_far, a, b, w0, a0):
    _, g = bend(a, a0 - a_far)
    return ((w0 - w) * jnp.maximum(c, 0.0) - b) * g


def upper_carry(w, a, a_far, forth, w_last, a_last, c_last):
    _, g = bend(a, a_far - a_last)
    return (forth - (w - w_last) * jnp.minimum(c_last, 0.0)) * g


def sweep(g, w, a, c, prev, after, a_low, a_high, w_low, w_high, c_low, r_low, r_high):
    t, bent = bend(a, after(a, a_high) - prev(a, a_low))
    below = prev(c, c_low)
    forth = (after(w, w_high) - w) * jnp.maximum(c, 0.0)
    back = (w - prev(w, w_low)) * jnp.minimum(below, 0.0)
    apart = forth - back
    r = apart * bent
    own = g + w * (c - below) + (forth + back) + apart * ((0.5 - a) * t)
    return own + (prev(r, r_low) - after(r, r_high))


def shifts(shape, dim):
    at = lax.broadcasted_iota(jnp.int32, shape, dim)
    length = shape[dim]

    def prev(value, edge):
        return jnp.where(at == 0, edge, pltpu.roll(value, 1, dim))

    def after(value, edge):
        return jnp.where(at == length - 1, edge, pltpu.roll(value, length - 1, dim))

    return prev, after


def fold(planes, rows, lanes):
    per = lanes // (slot * planes)
    return per if per >= 1 and rows % (8 * per) == 0 else 1


def z_pack(size, cot, opened, a_ref, c_ref, *out):
    planes, rows, lanes = a_ref.shape
    per = fold(planes, rows, lanes)
    step = rows // per
    at = lax.broadcasted_iota(jnp.int32, (rows, lanes), 1)
    totals = [None] * len(out)
    for x in range(planes):
        w = cot[x] * opened[x].astype(jnp.float32)
        a, c = a_ref[x], c_ref[x]
        w1 = pltpu.roll(w, 1, 1)
        back = (w - w1) * jnp.minimum(pltpu.roll(c, 1, 1), 0.0)
        forth = (pltpu.roll(w, lanes - 1, 1) - w) * jnp.maximum(c, 0.0)
        up = jnp.where(
            at < 2,
            jnp.where(at == 0, w1, pltpu.roll(c, 2, 1)),
            jnp.where(at < 4, pltpu.roll(a, 4, 1), pltpu.roll(back, 5, 1)),
        )
        down = jnp.where(
            at == 0, w, jnp.where(at < 3, pltpu.roll(a, 1, 1), pltpu.roll(forth, 3, 1))
        )
        for n, message in enumerate(to_send("gz", size, up, down)):
            message = jnp.where(at < 5, message, 0.0)
            total = totals[n]
            for r in range(per):
                part = message[r * step : (r + 1) * step]
                move = slot * (x + planes * r)
                part = pltpu.roll(part, move, 1) if move else part
                total = part if total is None else total + part
            totals[n] = total
    for ref, total in zip(out, totals):
        ref[...] = total


def z_unpack(message, x, planes, rows, lanes):
    per = fold(planes, rows, lanes)
    parts = []
    for r in range(per):
        move = slot * (x + planes * r)
        parts.append(pltpu.roll(message, lanes - move, 1) if move else message)
    return jnp.concatenate(parts, axis=0)


def z_sweep(sizes, cot, opened, az, cz, ay, cy, *rest):
    n_in = min(sizes[2] - 1, 2)
    messages, (g_ref, *out) = [m[...] for m in rest[:n_in]], rest[n_in:]
    planes, rows, lanes = az.shape
    prev, after = shifts((rows, lanes), 1)
    low_all, high_all = received("gz", sizes[2], messages, az[0])
    tile = lax.broadcasted_iota(jnp.int32, (8, lanes), 0)
    for x in range(planes):
        mask = opened[x].astype(jnp.float32)
        g = cot[x]
        w, a, c = mask * g, az[x], cz[x]
        low = z_unpack(low_all, x, planes, rows, lanes)
        high = z_unpack(high_all, x, planes, rows, lanes)
        lo = [low[:, v : v + 1] for v in range(5)]
        hi = [high[:, v : v + 1] for v in range(4)]
        r_low = lower_carry(*lo, w[:, 0:1], a[:, 0:1])
        r_high = upper_carry(*hi, w[:, lanes - 1 :], a[:, lanes - 1 :], c[:, lanes - 1 :])
        g = sweep(g, w, a, c, prev, after, lo[3], hi[1], lo[0], hi[0], lo[1], r_low, r_high)
        g_ref[x] = g
        if not out:
            continue
        first, last = (mask * g)[:8], (mask * g)[rows - 8 :]
        a_first, a_last = ay[x, :8], ay[x, rows - 8 :]
        c_first, c_last = cy[x, :8], cy[x, rows - 8 :]
        back = (last - pltpu.roll(last, 1, 0)) * jnp.minimum(pltpu.roll(c_last, 1, 0), 0.0)
        forth = (pltpu.roll(first, 7, 0) - first) * jnp.maximum(c_first, 0.0)
        up = jnp.where(
            tile < 2,
            jnp.where(tile == 0, pltpu.roll(last, 1, 0), pltpu.roll(c_last, 2, 0)),
            jnp.where(tile < 4, pltpu.roll(a_last, 4, 0), pltpu.roll(back, 5, 0)),
        )
        down = jnp.where(
            tile == 0,
            first,
            jnp.where(tile < 3, pltpu.roll(a_first, 1, 0), pltpu.roll(forth, 3, 0)),
        )
        for ref, message in zip(out, to_send("gy", sizes[1], up, down)):
            ref[x] = message


def y_sweep(sizes, g_in, opened, ay, cy, ax, cx, *rest):
    n_in = min(sizes[1] - 1, 2)
    messages, (g_ref, *out) = rest[:n_in], rest[n_in:]
    planes, rows, lanes = ay.shape
    prev, after = shifts((rows, lanes), 0)
    ws = []
    for x in range(planes):
        mask = opened[x].astype(jnp.float32)
        g = g_in[x]
        w, a, c = mask * g, ay[x], cy[x]
        low, high = received("gy", sizes[1], [m[x] for m in messages], a[:8])
        lo = [low[v : v + 1] for v in range(5)]
        hi = [high[v : v + 1] for v in range(4)]
        r_low = lower_carry(*lo, w[0:1], a[0:1])
        r_high = upper_carry(*hi, w[rows - 1 :], a[rows - 1 :], c[rows - 1 :])
        g = sweep(g, w, a, c, prev, after, lo[3], hi[1], lo[0], hi[0], lo[1], r_low, r_high)
        g_ref[x] = g
        ws.append(mask * g)
    if out:
        back = (ws[-1] - ws[-2]) * jnp.minimum(cx[planes - 2], 0.0)
        forth = (ws[1] - ws[0]) * jnp.maximum(cx[0], 0.0)
        for v, (up, down) in enumerate(((ws[-1], ws[0]), (back, forth))):
            for ref, message in zip(out, to_send("gx", sizes[0], up, down)):
                ref[v] = message


def x_fields(sizes, ax, cx, *out):
    planes = ax.shape[0]
    pairs = ((ax[planes - 2], ax[0]), (ax[planes - 1], ax[1]), (cx[planes - 1], cx[0]))
    for v, (up, down) in enumerate(pairs):
        for ref, message in zip(out, to_send("gx", sizes[0], up, down)):
            ref[v] = message


def x_sweep(sizes, g_in, opened, ax, cx, *rest):
    n_in = min(sizes[0] - 1, 2)
    fields, late, (out,) = rest[:n_in], rest[n_in : 2 * n_in], rest[2 * n_in :]
    planes = ax.shape[0]
    like = ax[0]
    (f0, h0), (f1, h1), (c_low, _) = (
        received("gx", sizes[0], [m[v] for m in fields], like) for v in range(3)
    )
    (w_low, w_high), (back, forth) = (
        received("gx", sizes[0], [m[v] for m in late], like) for v in range(2)
    )
    g = [g_in[x] for x in range(planes)]
    w = [opened[x].astype(jnp.float32) * g[x] for x in range(planes)]
    a = [ax[x] for x in range(planes)]
    c = [cx[x] for x in range(planes)]
    last = planes - 1
    r = [lower_carry(w_low, c_low, f0, f1, back, w[0], a[0])]
    own = []
    for x in range(planes):
        below = c[x - 1] if x else c_low
        t, bent = bend(a[x], (a[x + 1] if x < last else h0) - (a[x - 1] if x else f1))
        forth_x = ((w[x + 1] if x < last else w_high) - w[x]) * jnp.maximum(c[x], 0.0)
        back_x = (w[x] - (w[x - 1] if x else w_low)) * jnp.minimum(below, 0.0)
        apart = forth_x - back_x
        r.append(apart * bent)
        own.append(
            g[x] + w[x] * (c[x] - below) + (forth_x + back_x) + apart * ((0.5 - a[x]) * t)
        )
    r.append(upper_carry(w_high, h0, h1, forth, w[last], a[last], c[last]))
    for x in range(planes):
        out[x] = own[x] + (r[x] - r[x + 2])


def call(body, out, *args, name):
    shapes = [jax.ShapeDtypeStruct(shape, jnp.float32) for shape in out]
    return pl.pallas_call(
        body,
        out_shape=shapes,
        in_specs=[pl.BlockSpec(memory_space=pltpu.VMEM)] * len(args),
        out_specs=[pl.BlockSpec(memory_space=pltpu.VMEM)] * len(shapes),
        compiler_params=pltpu.CompilerParams(vmem_limit_bytes=8 * 2**20),
        name=name,
    )(*args)


def per_device(sizes, cot, ax, ay, az, cx, cy, cz, opened):
    x_rounds, y_rounds, z_rounds = (pair_rounds(sizes, d) for d in range(3))
    block = az.shape
    planes, rows, lanes = block
    swap = lambda value, perm: lax.ppermute(value, AXES, perm)
    packed = (rows // fold(planes, rows, lanes), lanes)
    z_out = call(
        functools.partial(z_pack, sizes[2]),
        [packed] * len(z_rounds),
        cot, opened, az, cz,
        name="z_pack",
    )
    z_in = [swap(m, p) for m, p in zip(z_out, z_rounds)]
    fields = call(
        functools.partial(x_fields, sizes), [(3, rows, lanes)] * len(x_rounds), ax, cx, name="x_fields"
    )
    fields = [swap(m, p) for m, p in zip(fields, x_rounds)]
    g, *y_out = call(
        functools.partial(z_sweep, sizes),
        [block] + [(planes, 8, lanes)] * len(y_rounds),
        cot, opened, az, cz, ay, cy, *z_in,
        name="z_sweep",
    )
    y_in = [swap(m, p) for m, p in zip(y_out, y_rounds)]
    g, *x_out = call(
        functools.partial(y_sweep, sizes),
        [block] + [(2, rows, lanes)] * len(x_rounds),
        g, opened, ay, cy, ax, cx, *y_in,
        name="y_sweep",
    )
    x_in = [swap(m, p) for m, p in zip(x_out, x_rounds)]
    (g,) = call(
        functools.partial(x_sweep, sizes), [block], g, opened, ax, cx, *fields, *x_in, name="x_sweep"
    )
    return g


def solution(mesh):
    sizes = tuple(mesh.shape[axis] for axis in AXES)
    placed = P(*AXES)
    return jax.shard_map(
        functools.partial(per_device, sizes),
        mesh=mesh,
        in_specs=(placed,) * 8,
        out_specs=placed,
        check_vma=False,
    )
```

```python
import functools

import jax
import jax.numpy as jnp
from jax import lax
from jax.experimental import pallas as pl
from jax.experimental.pallas import tpu as pltpu
from jax.sharding import PartitionSpec as P

sharpness = 3.5
slot = 8
AXES = ("gx", "gy", "gz")


def pair_rounds(sizes, along):
    size = sizes[along]
    if size == 1:
        return []
    assert size % 2 == 0

    def perm(partner):
        pairs = []
        for i in range(sizes[0]):
            for j in range(sizes[1]):
                for k in range(sizes[2]):
                    a, b, c = partner(i, j, k)
                    pairs.append(
                        ((i * sizes[1] + j) * sizes[2] + k, (a * sizes[1] + b) * sizes[2] + c)
                    )
        return pairs

    def even(*at):
        at = list(at)
        at[along] ^= 1
        return at

    def odd(*at):
        at = list(at)
        if 0 < at[along] < size - 1:
            at[along] = (at[along] - 1) ^ 1
            at[along] += 1
        elif along != 0 and sizes[0] % 2 == 0:
            at[0] ^= 1
        else:
            at[along] = size - 1 - at[along]
        return at

    return [perm(even)] if size == 2 else [perm(even), perm(odd)]


def roles(axis, size):
    at = lax.axis_index(axis)
    return lax.rem(at, 2) == 0, at > 0, at < size - 1


def to_send(axis, size, up, down):
    if size == 1:
        return []
    even, _, _ = roles(axis, size)
    first = jnp.where(even, up, down)
    return [first] if size == 2 else [first, jnp.where(even, down, up)]


def received(axis, size, messages, like):
    if size == 1:
        return jnp.zeros_like(like), jnp.zeros_like(like)
    even, has_low, has_high = roles(axis, size)
    first, second = messages[0], messages[-1]
    low = jnp.where(even, second, first)
    high = jnp.where(even, first, second)
    return jnp.where(has_low, low, 0.0), jnp.where(has_high, high, 0.0)


def bend(a, difference):
    t = jnp.tanh(sharpness * difference)
    return t, 0.5 * sharpness * a * (1.0 - a) * (1.0 - t * t)


def lower_carry(w, c, a_far, a, b, w0, a0):
    _, g = bend(a, a0 - a_far)
    return ((w0 - w) * jnp.maximum(c, 0.0) - b) * g


def upper_carry(w, a, a_far, forth, w_last, a_last, c_last):
    _, g = bend(a, a_far - a_last)
    return (forth - (w - w_last) * jnp.minimum(c_last, 0.0)) * g


def sweep(g, w, a, c, prev, after, a_low, a_high, w_low, w_high, c_low, r_low, r_high):
    t, bent = bend(a, after(a, a_high) - prev(a, a_low))
    below = prev(c, c_low)
    forth = (after(w, w_high) - w) * jnp.maximum(c, 0.0)
    back = (w - prev(w, w_low)) * jnp.minimum(below, 0.0)
    apart = forth - back
    r = apart * bent
    own = g + w * (c - below) + (forth + back) + apart * ((0.5 - a) * t)
    return own + (prev(r, r_low) - after(r, r_high))


def shifts(shape, dim):
    at = lax.broadcasted_iota(jnp.int32, shape, dim)
    length = shape[dim]

    def prev(value, edge):
        return jnp.where(at == 0, edge, pltpu.roll(value, 1, dim))

    def after(value, edge):
        return jnp.where(at == length - 1, edge, pltpu.roll(value, length - 1, dim))

    return prev, after


def fold(planes, rows, lanes):
    per = lanes // (slot * planes)
    return per if per >= 1 and rows % (8 * per) == 0 else 1


def edge_lanes(shape, lanes):
    at = lax.broadcasted_iota(jnp.int32, shape, 1)
    return at, lax.rem(at, slot)


def z_pack(size, planes, rows, lanes, cot_in, opened_in, a_in, c_in, *out):
    cot, opened, a_ref, c_ref, w_ref, edge_ref, *out, sems = out
    copies = [
        pltpu.make_async_copy(src, dst, sems.at[n])
        for n, (src, dst) in enumerate(
            ((cot_in, cot), (opened_in, opened), (a_in, a_ref), (c_in, c_ref))
        )
    ]
    for copy in copies:
        copy.start()
    for copy in copies:
        copy.wait()
    per = fold(planes, rows, lanes)
    step = rows // per
    at, place = edge_lanes((rows, lanes), lanes)
    near = (at < 2) | (at >= lanes - 2)
    totals = [None] * 3
    for x in range(planes):
        w = cot[x] * opened[x].astype(jnp.float32)
        w_ref[x] = w
        for n, field in enumerate((w, a_ref[x], c_ref[x])):
            field = jnp.where(near, field, 0.0)
            for r in range(per):
                move = slot * (x + planes * r)
                part = field[r * step : (r + 1) * step]
                part = pltpu.roll(part, move, 1) if move else part
                totals[n] = part if totals[n] is None else totals[n] + part
    for n in range(3):
        edge_ref[n] = totals[n]
    _, place = edge_lanes((step, lanes), lanes)
    ends = [jnp.where(place >= slot - 2, total, 0.0) for total in totals]
    starts = [jnp.where(place < 2, total, 0.0) for total in totals]
    up = sum(pltpu.roll(end, 2 + 2 * n, 1) for n, end in enumerate(ends))
    down = sum(pltpu.roll(start, 2 * n, 1) if n else start for n, start in enumerate(starts))
    for ref, message in zip(out, to_send("gz", size, up, down)):
        ref[...] = message


def z_inner(g_ref, w_ref, a_ref, c_ref, out):
    planes, rows, lanes = a_ref.shape
    at = lax.broadcasted_iota(jnp.int32, (rows, lanes), 1)
    inside = (at > 0) & (at < lanes - 1)
    prev = lambda value: pltpu.roll(value, 1, 1)
    after = lambda value: pltpu.roll(value, lanes - 1, 1)
    for x in range(planes):
        w, a, c = w_ref[x], a_ref[x], c_ref[x]
        t, bent = bend(a, after(a) - prev(a))
        below = prev(c)
        forth = (after(w) - w) * jnp.maximum(c, 0.0)
        back = (w - prev(w)) * jnp.minimum(below, 0.0)
        apart = jnp.where(inside, forth - back, 0.0)
        own = jnp.where(inside, w * (c - below) + (forth + back), 0.0) + apart * ((0.5 - a) * t)
        r = apart * bent
        out[x] = g_ref[x] + own + (prev(r) - after(r))


def z_ends(edges, low, high, lanes):
    shift = lambda value, by: pltpu.roll(value, by % lanes, 1)
    w, a, c = edges
    _, place = edge_lanes(w.shape, lanes)
    w0, w1, a0, a1, c0 = w, shift(w, -1), a, shift(a, -1), c
    w_far, w_low, a_far, a_low, c_far, c_low = (shift(low, -v) if v else low for v in range(6))
    r_low = lower_carry(w_low, c_low, a_far, a_low, (w_low - w_far) * jnp.minimum(c_far, 0.0), w0, a0)
    forth = (w1 - w0) * jnp.maximum(c0, 0.0)
    back = (w0 - w_low) * jnp.minimum(c_low, 0.0)
    t, bent = bend(a0, a1 - a_low)
    first = w0 * (c0 - c_low) + (forth + back) + (forth - back) * ((0.5 - a0) * t) + r_low
    second = (forth - back) * bent
    w1, a1, c1 = shift(w, 1), shift(a, 1), shift(c, 1)
    w0, a0, c0 = shift(w, 2), shift(a, 2), shift(c, 2)
    w_high, w_far, a_high, a_far, c_high = (shift(high, -v) if v else high for v in range(5))
    r_high = upper_carry(w_high, a_high, a_far, (w_far - w_high) * jnp.maximum(c_high, 0.0), w1, a1, c1)
    forth = (w_high - w1) * jnp.maximum(c1, 0.0)
    back = (w1 - w0) * jnp.minimum(c0, 0.0)
    t, bent = bend(a1, a_high - a0)
    last = w1 * (c1 - c0) + (forth + back) + (forth - back) * ((0.5 - a1) * t) - r_high
    before = (back - forth) * bent
    ends = jnp.where(place == 0, first, jnp.where(place == 1, shift(second, 1), 0.0))
    return jnp.where(
        place == slot - 1, shift(last, -1), jnp.where(place == slot - 2, shift(before, -2), ends)
    )


def z_sweep(sizes, partial, edges, opened, ay, cy, *rest):
    n_in = min(sizes[2] - 1, 2)
    messages, (g_ref, *out) = [m[...] for m in rest[:n_in]], rest[n_in:]
    planes, rows, lanes = ay.shape
    low, high = received("gz", sizes[2], messages, edges[0])
    ends = z_ends([edges[n] for n in range(3)], low, high, lanes)
    at = lax.broadcasted_iota(jnp.int32, (rows, lanes), 1)
    near = (at < 2) | (at >= lanes - 2)
    per = fold(planes, rows, lanes)
    tile = lax.broadcasted_iota(jnp.int32, (8, lanes), 0)
    for x in range(planes):
        parts = []
        for r in range(per):
            move = slot * (x + planes * r)
            parts.append(pltpu.roll(ends, lanes - move, 1) if move else ends)
        g = partial[x] + jnp.where(near, jnp.concatenate(parts, axis=0), 0.0)
        g_ref[x] = g
        if not out:
            continue
        mask = opened[x].astype(jnp.float32)
        first, last = (mask * g)[:8], (mask * g)[rows - 8 :]
        a_first, a_last = ay[x, :8], ay[x, rows - 8 :]
        c_first, c_last = cy[x, :8], cy[x, rows - 8 :]
        back = (last - pltpu.roll(last, 1, 0)) * jnp.minimum(pltpu.roll(c_last, 1, 0), 0.0)
        forth = (pltpu.roll(first, 7, 0) - first) * jnp.maximum(c_first, 0.0)
        up = jnp.where(
            tile < 2,
            jnp.where(tile == 0, pltpu.roll(last, 1, 0), pltpu.roll(c_last, 2, 0)),
            jnp.where(tile < 4, pltpu.roll(a_last, 4, 0), pltpu.roll(back, 5, 0)),
        )
        down = jnp.where(
            tile == 0,
            first,
            jnp.where(tile < 3, pltpu.roll(a_first, 1, 0), pltpu.roll(forth, 3, 0)),
        )
        for ref, message in zip(out, to_send("gy", sizes[1], up, down)):
            ref[x] = message


def y_sweep(sizes, g_in, opened, ay, cy, ax, cx, *rest):
    n_in = min(sizes[1] - 1, 2)
    messages, (g_ref, *out) = rest[:n_in], rest[n_in:]
    planes, rows, lanes = ay.shape
    prev, after = shifts((rows, lanes), 0)
    ws = []
    for x in range(planes):
        mask = opened[x].astype(jnp.float32)
        g = g_in[x]
        w, a, c = mask * g, ay[x], cy[x]
        low, high = received("gy", sizes[1], [m[x] for m in messages], a[:8])
        lo = [low[v : v + 1] for v in range(5)]
        hi = [high[v : v + 1] for v in range(4)]
        r_low = lower_carry(*lo, w[0:1], a[0:1])
        r_high = upper_carry(*hi, w[rows - 1 :], a[rows - 1 :], c[rows - 1 :])
        g = sweep(g, w, a, c, prev, after, lo[3], hi[1], lo[0], hi[0], lo[1], r_low, r_high)
        g_ref[x] = g
        ws.append(mask * g)
    if out:
        back = (ws[-1] - ws[-2]) * jnp.minimum(cx[planes - 2], 0.0)
        forth = (ws[1] - ws[0]) * jnp.maximum(cx[0], 0.0)
        pairs = (
            (ws[-1], ws[0]),
            (back, forth),
            (ax[planes - 2], ax[0]),
            (ax[planes - 1], ax[1]),
            (cx[planes - 1], cx[0]),
        )
        for v, (up, down) in enumerate(pairs):
            for ref, message in zip(out, to_send("gx", sizes[0], up, down)):
                ref[v] = message


def x_sweep(sizes, g_in, opened, ax, cx, *rest):
    n_in = min(sizes[0] - 1, 2)
    messages, (out,) = rest[:n_in], rest[n_in:]
    planes = ax.shape[0]
    like = ax[0]
    (w_low, w_high), (back, forth), (f0, h0), (f1, h1), (c_low, _) = (
        received("gx", sizes[0], [m[v] for m in messages], like) for v in range(5)
    )
    g = [g_in[x] for x in range(planes)]
    w = [opened[x].astype(jnp.float32) * g[x] for x in range(planes)]
    a = [ax[x] for x in range(planes)]
    c = [cx[x] for x in range(planes)]
    last = planes - 1
    r = [lower_carry(w_low, c_low, f0, f1, back, w[0], a[0])]
    own = []
    for x in range(planes):
        below = c[x - 1] if x else c_low
        t, bent = bend(a[x], (a[x + 1] if x < last else h0) - (a[x - 1] if x else f1))
        forth_x = ((w[x + 1] if x < last else w_high) - w[x]) * jnp.maximum(c[x], 0.0)
        back_x = (w[x] - (w[x - 1] if x else w_low)) * jnp.minimum(below, 0.0)
        apart = forth_x - back_x
        r.append(apart * bent)
        own.append(
            g[x] + w[x] * (c[x] - below) + (forth_x + back_x) + apart * ((0.5 - a[x]) * t)
        )
    r.append(upper_carry(w_high, h0, h1, forth, w[last], a[last], c[last]))
    for x in range(planes):
        out[x] = own[x] + (r[x] - r[x + 2])


def call(body, out, *args, name, source=pltpu.VMEM, scratch=(), limit=8):
    shapes = [jax.ShapeDtypeStruct(o, jnp.float32) if isinstance(o, tuple) else o for o in out]
    return pl.pallas_call(
        body,
        out_shape=shapes,
        in_specs=[pl.BlockSpec(memory_space=source)] * len(args),
        out_specs=[pl.BlockSpec(memory_space=pltpu.VMEM)] * len(shapes),
        scratch_shapes=scratch,
        compiler_params=pltpu.CompilerParams(vmem_limit_bytes=limit * 2**20),
        name=name,
    )(*args)


def per_device(sizes, cot, ax, ay, az, cx, cy, cz, opened):
    x_rounds, y_rounds, z_rounds = (pair_rounds(sizes, d) for d in range(3))
    block = az.shape
    planes, rows, lanes = block
    swap = lambda value, perm: lax.ppermute(value, AXES, perm)
    packed = (rows // fold(planes, rows, lanes), lanes)
    cot, opened, az, cz, w, edges, *z_out = call(
        functools.partial(z_pack, sizes[2], planes, rows, lanes),
        [block, jax.ShapeDtypeStruct(block, jnp.int32), block, block, block, (3, *packed)]
        + [packed] * len(z_rounds),
        *(pltpu.with_memory_space_constraint(v, pltpu.HBM) for v in (cot, opened, az, cz)),
        name="z_pack", source=pltpu.HBM, limit=8, scratch=[pltpu.SemaphoreType.DMA((4,))],
    )
    z_in = [swap(m, p) for m, p in zip(z_out, z_rounds)]
    (partial,) = call(z_inner, [block], cot, w, az, cz, name="z_inner")
    g, *y_out = call(
        functools.partial(z_sweep, sizes),
        [block] + [(planes, 8, lanes)] * len(y_rounds),
        partial, edges, opened, ay, cy, *z_in,
        name="z_sweep",
    )
    y_in = [swap(m, p) for m, p in zip(y_out, y_rounds)]
    g, *x_out = call(
        functools.partial(y_sweep, sizes),
        [block] + [(5, rows, lanes)] * len(x_rounds),
        g, opened, ay, cy, ax, cx, *y_in,
        name="y_sweep",
    )
    x_in = [swap(m, p) for m, p in zip(x_out, x_rounds)]
    (g,) = call(
        functools.partial(x_sweep, sizes), [block], g, opened, ax, cx, *x_in, name="x_sweep"
    )
    return g


def solution(mesh):
    sizes = tuple(mesh.shape[axis] for axis in AXES)
    placed = P(*AXES)
    return jax.shard_map(
        functools.partial(per_device, sizes),
        mesh=mesh,
        in_specs=(placed,) * 8,
        out_specs=placed,
        check_vma=False,
    )
```

```python
import functools

import jax
import jax.numpy as jnp
from jax import lax
from jax.experimental import pallas as pl
from jax.experimental.pallas import tpu as pltpu
from jax.sharding import PartitionSpec as P

sharpness = 3.5
slot = 8
AXES = ("gx", "gy", "gz")


def pair_rounds(sizes, along):
    size = sizes[along]
    if size == 1:
        return []
    assert size % 2 == 0

    def perm(partner):
        pairs = []
        for i in range(sizes[0]):
            for j in range(sizes[1]):
                for k in range(sizes[2]):
                    a, b, c = partner(i, j, k)
                    pairs.append(
                        ((i * sizes[1] + j) * sizes[2] + k, (a * sizes[1] + b) * sizes[2] + c)
                    )
        return pairs

    def even(*at):
        at = list(at)
        at[along] ^= 1
        return at

    def odd(*at):
        at = list(at)
        if 0 < at[along] < size - 1:
            at[along] = (at[along] - 1) ^ 1
            at[along] += 1
        elif along != 0 and sizes[0] % 2 == 0:
            at[0] ^= 1
        elif along == 0 and sizes[1] % 2 == 0:
            at[1] ^= 1
        else:
            at[along] = size - 1 - at[along]
        return at

    return [perm(even)] if size == 2 else [perm(even), perm(odd)]


def roles(axis, size):
    at = lax.axis_index(axis)
    return lax.rem(at, 2) == 0, at > 0, at < size - 1


def to_send(axis, size, up, down):
    if size == 1:
        return []
    even, _, _ = roles(axis, size)
    first = jnp.where(even, up, down)
    return [first] if size == 2 else [first, jnp.where(even, down, up)]


def received(axis, size, messages, like):
    if size == 1:
        return jnp.zeros_like(like), jnp.zeros_like(like)
    even, has_low, has_high = roles(axis, size)
    first, second = messages[0], messages[-1]
    low = jnp.where(even, second, first)
    high = jnp.where(even, first, second)
    return jnp.where(has_low, low, 0.0), jnp.where(has_high, high, 0.0)


def bend(a, difference):
    t = jnp.tanh(sharpness * difference)
    return t, 0.5 * sharpness * a * (1.0 - a) * (1.0 - t * t)


def low_end(low, w0, w1, a0, a1, c0):
    w_far, w_low, a_far, a_low, c_far, c_low = low
    _, bent = bend(a_low, a0 - a_far)
    across = w0 - w_low
    r_low = (across * jnp.maximum(c_low, 0.0) - (w_low - w_far) * jnp.minimum(c_far, 0.0)) * bent
    forth = (w1 - w0) * jnp.maximum(c0, 0.0)
    back = across * jnp.minimum(c_low, 0.0)
    t, bent = bend(a0, a1 - a_low)
    first = w0 * (c0 - c_low) + (forth + back) + (forth - back) * ((0.5 - a0) * t) + r_low
    return first, (forth - back) * bent


def high_end(high, w0, w1, a0, a1, c0, c1):
    w_high, w_far, a_high, a_far, c_high = high
    _, bent = bend(a_high, a_far - a1)
    across = w_high - w1
    r_high = ((w_far - w_high) * jnp.maximum(c_high, 0.0) - across * jnp.minimum(c1, 0.0)) * bent
    forth = across * jnp.maximum(c1, 0.0)
    back = (w1 - w0) * jnp.minimum(c0, 0.0)
    t, bent = bend(a1, a_high - a0)
    last = w1 * (c1 - c0) + (forth + back) + (forth - back) * ((0.5 - a1) * t) - r_high
    return last, (back - forth) * bent


def interior(g, w, a, c, dim):
    length = a.shape[dim]
    at = lax.broadcasted_iota(jnp.int32, a.shape, dim)
    inside = (at > 0) & (at < length - 1)
    prev = lambda value: pltpu.roll(value, 1, dim)
    after = lambda value: pltpu.roll(value, length - 1, dim)
    t, bent = bend(a, after(a) - prev(a))
    below = prev(c)
    forth = (after(w) - w) * jnp.maximum(c, 0.0)
    back = (w - prev(w)) * jnp.minimum(below, 0.0)
    apart = jnp.where(inside, forth - back, 0.0)
    own = jnp.where(inside, w * (c - below) + (forth + back), 0.0) + apart * ((0.5 - a) * t)
    r = apart * bent
    return g + own + (prev(r) - after(r))


def fold(planes, rows, lanes):
    per = lanes // (slot * planes)
    return per if per >= 1 and rows % (8 * per) == 0 else 1


def edge_lanes(shape, lanes):
    at = lax.broadcasted_iota(jnp.int32, shape, 1)
    return at, lax.rem(at, slot)


def z_pack(size, planes, rows, lanes, cot_in, opened_in, a_in, c_in, *out):
    cot, opened, a_ref, c_ref, w_ref, edge_ref, *out, sems = out
    copies = [
        pltpu.make_async_copy(src, dst, sems.at[n])
        for n, (src, dst) in enumerate(
            ((cot_in, cot), (opened_in, opened), (a_in, a_ref), (c_in, c_ref))
        )
    ]
    for copy in copies:
        copy.start()
    for copy in copies:
        copy.wait()
    per = fold(planes, rows, lanes)
    step = rows // per
    at, place = edge_lanes((rows, lanes), lanes)
    near = (at < 2) | (at >= lanes - 2)
    totals = [None] * 3
    for x in range(planes):
        w = cot[x] * opened[x].astype(jnp.float32)
        w_ref[x] = w
        for n, field in enumerate((w, a_ref[x], c_ref[x])):
            field = jnp.where(near, field, 0.0)
            for r in range(per):
                move = slot * (x + planes * r)
                part = field[r * step : (r + 1) * step]
                part = pltpu.roll(part, move, 1) if move else part
                totals[n] = part if totals[n] is None else totals[n] + part
    for n in range(3):
        edge_ref[n] = totals[n]
    _, place = edge_lanes((step, lanes), lanes)
    ends = [jnp.where(place >= slot - 2, total, 0.0) for total in totals]
    starts = [jnp.where(place < 2, total, 0.0) for total in totals]
    up = sum(pltpu.roll(end, 2 + 2 * n, 1) for n, end in enumerate(ends))
    down = sum(pltpu.roll(start, 2 * n, 1) if n else start for n, start in enumerate(starts))
    for ref, message in zip(out, to_send("gz", size, up, down)):
        ref[...] = message


def z_inner(g_ref, w_ref, a_ref, c_ref, *rest):
    *sources, out = rest[: len(rest) // 2]
    *targets, sems = rest[len(rest) // 2 :]
    copies = [
        pltpu.make_async_copy(src, dst, sems.at[n]) for n, (src, dst) in enumerate(zip(sources, targets))
    ]
    for copy in copies:
        copy.start()
    for x in range(a_ref.shape[0]):
        out[x] = interior(g_ref[x], w_ref[x], a_ref[x], c_ref[x], 1)
    for copy in copies:
        copy.wait()


def z_ends(edges, low, high, lanes):
    shift = lambda value, by: pltpu.roll(value, by % lanes, 1)
    w, a, c = edges
    _, place = edge_lanes(w.shape, lanes)
    low = [shift(low, -v) if v else low for v in range(6)]
    first, second = low_end(low, w, shift(w, -1), a, shift(a, -1), c)
    high = [shift(high, -v) if v else high for v in range(5)]
    last, before = high_end(
        high, shift(w, 2), shift(w, 1), shift(a, 2), shift(a, 1), shift(c, 2), shift(c, 1)
    )
    ends = jnp.where(place == 0, first, jnp.where(place == 1, shift(second, 1), 0.0))
    return jnp.where(
        place == slot - 1, shift(last, -1), jnp.where(place == slot - 2, shift(before, -2), ends)
    )


def z_sweep(sizes, partial, edges, opened, ay, cy, *rest):
    n_in = min(sizes[2] - 1, 2)
    messages, (g_ref, *out) = [m[...] for m in rest[:n_in]], rest[n_in:]
    planes, rows, lanes = ay.shape
    low, high = received("gz", sizes[2], messages, edges[0])
    ends = z_ends([edges[n] for n in range(3)], low, high, lanes)
    at = lax.broadcasted_iota(jnp.int32, (rows, lanes), 1)
    near = (at < 2) | (at >= lanes - 2)
    per = fold(planes, rows, lanes)
    tile = lax.broadcasted_iota(jnp.int32, (8, lanes), 0)
    for x in range(planes):
        parts = []
        for r in range(per):
            move = slot * (x + planes * r)
            parts.append(pltpu.roll(ends, lanes - move, 1) if move else ends)
        g = partial[x] + jnp.where(near, jnp.concatenate(parts, axis=0), 0.0)
        g_ref[x] = g
        if not out:
            continue
        mask = opened[x].astype(jnp.float32)
        w = mask * g
        pick = lambda *tiles: jnp.where(tile < 2, tiles[0], jnp.where(tile < 4, tiles[1], tiles[2]))
        up = pick(
            *(
                pltpu.roll(field[rows - 8 :], by, 0)
                for field, by in ((w, 2), (ay[x], 4), (cy[x], 6))
            )
        )
        down = pick(w[:8], pltpu.roll(ay[x, :8], 2, 0), pltpu.roll(cy[x, :8], 4, 0))
        for ref, message in zip(out, to_send("gy", sizes[1], up, down)):
            ref[x] = message


def x_messages(w, ax, cx):
    planes = len(w)
    back = (w[-1] - w[-2]) * jnp.minimum(cx[planes - 2], 0.0)
    forth = (w[1] - w[0]) * jnp.maximum(cx[0], 0.0)
    return (w[-1], w[0]), (back, forth)


def y_inner(sizes, g_in, opened, ay, cy, ax, cx, partial, *out):
    planes = ay.shape[0]
    w = []
    for x in range(planes):
        mask = opened[x].astype(jnp.float32)
        g = interior(g_in[x], mask * g_in[x], ay[x], cy[x], 0)
        partial[x] = g
        w.append(mask * g)
    pairs = (
        *x_messages(w, ax, cx),
        (ax[planes - 2], ax[0]),
        (ax[planes - 1], ax[1]),
        (cx[planes - 1], cx[0]),
    )
    for v, (up, down) in enumerate(pairs):
        for ref, message in zip(out, to_send("gx", sizes[0], up, down)):
            ref[v] = message


def y_sweep(sizes, partial, g_in, opened, ay, cy, cx, *rest):
    n_in = min(sizes[1] - 1, 2)
    messages, (g_ref, *out) = rest[:n_in], rest[n_in:]
    planes, rows, lanes = ay.shape
    tile = lax.broadcasted_iota(jnp.int32, (8, lanes), 0)
    ws = []
    for x in range(planes):
        low, high = received("gy", sizes[1], [m[x] for m in messages], ay[x, :8])
        row = lambda ref, n: ref[x, n : n + 1]
        w = [opened[x, n : n + 1].astype(jnp.float32) * row(g_in, n) for n in (0, 1, rows - 2, rows - 1)]
        first, second = low_end(
            [low[v : v + 1] for v in range(6)], w[0], w[1], row(ay, 0), row(ay, 1), row(cy, 0)
        )
        last, before = high_end(
            [high[v : v + 1] for v in range(5)],
            w[2],
            w[3],
            *(row(ref, n) for ref in (ay, cy) for n in (rows - 2, rows - 1)),
        )
        top = partial[x, :8] + jnp.where(tile == 0, first, jnp.where(tile == 1, second, 0.0))
        bottom = partial[x, rows - 8 :] + jnp.where(
            tile == 7, last, jnp.where(tile == 6, before, 0.0)
        )
        g_ref[x, :8] = top
        g_ref[x, 8 : rows - 8] = partial[x, 8 : rows - 8]
        g_ref[x, rows - 8 :] = bottom
        mask = jnp.where(tile < 4, opened[x, :8], opened[x, rows - 8 :]).astype(jnp.float32)
        ws.append(mask * jnp.where(tile < 4, top, bottom))
    if out:
        c = [jnp.where(tile < 4, cx[x, :8], cx[x, rows - 8 :]) for x in range(planes)]
        for v, (up, down) in enumerate(x_messages(ws, None, c)):
            for ref, message in zip(out, to_send("gx", sizes[0], up, down)):
                ref[v] = message


def x_sweep(sizes, g_in, opened, ax, cx, *rest):
    n_in = min(sizes[0] - 1, 2)
    early, late, (out,) = rest[:n_in], rest[n_in : 2 * n_in], rest[2 * n_in :]
    planes, rows, lanes = ax.shape
    like = ax[0]
    tile = lax.broadcasted_iota(jnp.int32, (8, lanes), 0)

    def whole(n, v):
        if v > 1:
            return early[n][v]
        ends = late[n][v]
        top = jnp.where(tile < 2, ends, early[n][v, :8])
        bottom = jnp.where(tile >= 6, ends, early[n][v, rows - 8 :])
        return jnp.concatenate([top, early[n][v, 8 : rows - 8], bottom], axis=0)

    (w_low, w_high), (b_low, f_high), (f0, h0), (f1, h1), (c_low, _) = (
        received("gx", sizes[0], [whole(n, v) for n in range(n_in)], like) for v in range(5)
    )
    g = [g_in[x] for x in range(planes)]
    w = [opened[x].astype(jnp.float32) * g[x] for x in range(planes)]
    a = [f1] + [ax[x] for x in range(planes)] + [h0]
    c = [c_low] + [cx[x] for x in range(planes)]
    last = planes - 1
    _, bent = bend(f1, a[1] - f0)
    r = [((w[0] - w_low) * jnp.maximum(c_low, 0.0) - b_low) * bent]
    own = []
    for x in range(planes):
        t, bent = bend(a[x + 1], a[x + 2] - a[x])
        forth = ((w[x + 1] if x < last else w_high) - w[x]) * jnp.maximum(c[x + 1], 0.0)
        back = (w[x] - (w[x - 1] if x else w_low)) * jnp.minimum(c[x], 0.0)
        apart = forth - back
        r.append(apart * bent)
        own.append(
            g[x] + w[x] * (c[x + 1] - c[x]) + (forth + back) + apart * ((0.5 - a[x + 1]) * t)
        )
    _, bent = bend(h0, h1 - a[planes])
    r.append((f_high - (w_high - w[last]) * jnp.minimum(c[planes], 0.0)) * bent)
    for x in range(planes):
        out[x] = own[x] + (r[x] - r[x + 2])


def call(body, out, *args, name, loads=(), scratch=(), us=0.3, flops=0):
    shapes = [jax.ShapeDtypeStruct(o, jnp.float32) if isinstance(o, tuple) else o for o in out]
    loads = [pltpu.with_memory_space_constraint(v, pltpu.HBM) for v in loads]
    return pl.pallas_call(
        body,
        out_shape=shapes,
        in_specs=[pl.BlockSpec(memory_space=pltpu.VMEM)] * len(args)
        + [pl.BlockSpec(memory_space=pltpu.HBM)] * len(loads),
        out_specs=[pl.BlockSpec(memory_space=pltpu.VMEM)] * len(shapes),
        scratch_shapes=scratch,
        compiler_params=pltpu.CompilerParams(vmem_limit_bytes=8 * 2**20),
        cost_estimate=pl.CostEstimate(
            flops=flops, bytes_accessed=int(us * 3_690_000), transcendentals=0
        ),
        name=name,
    )(*args, *loads)


def per_device(sizes, cot, ax, ay, az, cx, cy, cz, opened):
    x_rounds, y_rounds, z_rounds = (pair_rounds(sizes, d) for d in range(3))
    block = az.shape
    planes, rows, lanes = block
    swap = lambda value, perm: lax.ppermute(value, AXES, perm)
    packed = (rows // fold(planes, rows, lanes), lanes)
    cot, opened, az, cz, w, edges, *z_out = call(
        functools.partial(z_pack, sizes[2], planes, rows, lanes),
        [block, jax.ShapeDtypeStruct(block, jnp.int32), block, block, block, (3, *packed)]
        + [packed] * len(z_rounds),
        loads=(cot, opened, az, cz),
        name="z_pack", scratch=[pltpu.SemaphoreType.DMA((4,))],
    )
    z_in = [swap(m, p) for m, p in zip(z_out, z_rounds)]
    partial, ax, ay, cx, cy = call(
        z_inner,
        [block] * 5,
        cot, w, az, cz,
        loads=(ax, ay, cx, cy),
        name="z_inner", scratch=[pltpu.SemaphoreType.DMA((4,))],
    )
    g, *y_out = call(
        functools.partial(z_sweep, sizes),
        [block] + [(planes, 8, lanes)] * len(y_rounds),
        partial, edges, opened, ay, cy, *z_in,
        name="z_sweep",
    )
    y_in = [swap(m, p) for m, p in zip(y_out, y_rounds)]
    partial, *x_out = call(
        functools.partial(y_inner, sizes),
        [block] + [(5, rows, lanes)] * len(x_rounds),
        g, opened, ay, cy, ax, cx,
        name="y_inner",
    )
    x_early = [swap(m, p) for m, p in zip(x_out, x_rounds)]
    g, *x_out = call(
        functools.partial(y_sweep, sizes),
        [block] + [(2, 8, lanes)] * len(x_rounds),
        partial, g, opened, ay, cy, cx, *y_in,
        name="y_sweep", flops=10000000000,
    )
    x_late = [swap(m, p) for m, p in zip(x_out, x_rounds)]
    (g,) = call(
        functools.partial(x_sweep, sizes), [block], g, opened, ax, cx, *x_early, *x_late, name="x_sweep"
    )
    return g


def solution(mesh):
    sizes = tuple(mesh.shape[axis] for axis in AXES)
    placed = P(*AXES)
    return jax.shard_map(
        functools.partial(per_device, sizes),
        mesh=mesh,
        in_specs=(placed,) * 8,
        out_specs=placed,
        check_vma=False,
    )
```

```python
import functools
import itertools

import jax
import jax.numpy as jnp
from jax import lax
from jax.experimental import pallas as pl
from jax.experimental.pallas import tpu as pltpu
from jax.sharding import PartitionSpec as P

sharpness = 3.5
slot = 8
AXES = ("gx", "gy", "gz")


def colours(sizes, along):
    return min(sizes[along] - 1, 3 if along == 2 else 2)


def turn_of(face, along, n):
    return (face + (1 if along == 0 else 0)) % n


def pair_rounds(sizes, along, aside=0):
    n = colours(sizes, along)

    def partner(at, turn):
        at = list(at)
        i = at[along]
        if turn_of(i, along, n) == turn and i + 1 < sizes[along]:
            at[along] += 1
        elif i > 0 and turn_of(i - 1, along, n) == turn:
            at[along] -= 1
        elif aside == along:
            at[along] = sizes[along] - 1 - i
        elif sizes[aside] % 2 == 0:
            at[aside] ^= 1
        return at

    places = list(itertools.product(*(range(size) for size in sizes)))
    flat = lambda at: (at[0] * sizes[1] + at[1]) * sizes[2] + at[2]
    return [[(flat(at), flat(partner(at, turn))) for at in places] for turn in range(n)]


def to_send(sizes, along, up, down):
    n, at = colours(sizes, along), lax.axis_index(AXES[along])
    if n <= 1:
        return [jnp.where(at == 0, up, down)] * n
    mine = turn_of(at, along, n)
    return [jnp.where((mine == turn) & (at < sizes[along] - 1), up, down) for turn in range(n)]


def received(sizes, along, messages, like):
    n, at = colours(sizes, along), lax.axis_index(AXES[along])
    if n == 0:
        return jnp.zeros_like(like), jnp.zeros_like(like)
    low = high = messages[0]
    for turn in range(1, n):
        low = jnp.where(turn_of(at + n - 1, along, n) == turn, messages[turn], low)
        high = jnp.where(turn_of(at, along, n) == turn, messages[turn], high)
    return jnp.where(at > 0, low, 0.0), jnp.where(at < sizes[along] - 1, high, 0.0)


def bend(a, difference):
    t = jnp.tanh(sharpness * difference)
    return t, 0.5 * sharpness * a * (1.0 - a) * (1.0 - t * t)


def low_end(low, w0, w1, a0, a1, c0):
    w_far, w_low, a_far, a_low, c_far, c_low = low
    _, bent = bend(a_low, a0 - a_far)
    across = w0 - w_low
    r_low = (across * jnp.maximum(c_low, 0.0) - (w_low - w_far) * jnp.minimum(c_far, 0.0)) * bent
    forth = (w1 - w0) * jnp.maximum(c0, 0.0)
    back = across * jnp.minimum(c_low, 0.0)
    t, bent = bend(a0, a1 - a_low)
    first = w0 * (c0 - c_low) + (forth + back) + (forth - back) * ((0.5 - a0) * t) + r_low
    return first, (forth - back) * bent


def high_end(high, w0, w1, a0, a1, c0, c1):
    w_high, w_far, a_high, a_far, c_high = high
    _, bent = bend(a_high, a_far - a1)
    across = w_high - w1
    r_high = ((w_far - w_high) * jnp.maximum(c_high, 0.0) - across * jnp.minimum(c1, 0.0)) * bent
    forth = across * jnp.maximum(c1, 0.0)
    back = (w1 - w0) * jnp.minimum(c0, 0.0)
    t, bent = bend(a1, a_high - a0)
    last = w1 * (c1 - c0) + (forth + back) + (forth - back) * ((0.5 - a1) * t) - r_high
    return last, (back - forth) * bent


def interior(g, w, a, c, dim):
    length = a.shape[dim]
    at = lax.broadcasted_iota(jnp.int32, a.shape, dim)
    inside = (at > 0) & (at < length - 1)
    prev = lambda value: pltpu.roll(value, 1, dim)
    after = lambda value: pltpu.roll(value, length - 1, dim)
    t, bent = bend(a, after(a) - prev(a))
    below = prev(c)
    forth = (after(w) - w) * jnp.maximum(c, 0.0)
    back = (w - prev(w)) * jnp.minimum(below, 0.0)
    apart = jnp.where(inside, forth - back, 0.0)
    own = jnp.where(inside, w * (c - below) + (forth + back), 0.0) + apart * ((0.5 - a) * t)
    r = apart * bent
    return g + own + (prev(r) - after(r))


def fold(planes, rows, lanes):
    per = lanes // (slot * planes)
    return per if per >= 1 and rows % (8 * per) == 0 else 1


def edge_lanes(shape, lanes):
    at = lax.broadcasted_iota(jnp.int32, shape, 1)
    return at, lax.rem(at, slot)


def z_pack(sizes, planes, rows, lanes, *refs):
    sources, targets, (w_ref, edge_ref, *out, sems) = refs[:4], refs[4:8], refs[8:]
    copies = [
        [
            pltpu.make_async_copy(src.at[x], dst.at[x], sems.at[n, x])
            for n, (src, dst) in enumerate(zip(sources, targets))
        ]
        for x in range(planes)
    ]
    for copy in itertools.chain(*copies):
        copy.start()
    cot, opened, a_ref, c_ref = targets
    per = fold(planes, rows, lanes)
    step = rows // per
    at, place = edge_lanes((rows, lanes), lanes)
    near = (at < 2) | (at >= lanes - 2)
    totals = [None] * 3
    for x in range(planes):
        for copy in copies[x]:
            copy.wait()
        w = cot[x] * opened[x].astype(jnp.float32)
        w_ref[x] = w
        for n, field in enumerate((w, a_ref[x], c_ref[x])):
            field = jnp.where(near, field, 0.0)
            for r in range(per):
                move = slot * (x + planes * r)
                part = field[r * step : (r + 1) * step]
                part = pltpu.roll(part, move, 1) if move else part
                totals[n] = part if totals[n] is None else totals[n] + part
    for n in range(3):
        edge_ref[n] = totals[n]
    _, place = edge_lanes((step, lanes), lanes)
    ends = [jnp.where(place >= slot - 2, total, 0.0) for total in totals]
    starts = [jnp.where(place < 2, total, 0.0) for total in totals]
    up = sum(pltpu.roll(end, 2 + 2 * n, 1) for n, end in enumerate(ends))
    down = sum(pltpu.roll(start, 2 * n, 1) if n else start for n, start in enumerate(starts))
    for ref, message in zip(out, to_send(sizes, 2, up, down)):
        ref[...] = message


def z_inner(g_ref, w_ref, a_ref, c_ref, out):
    for x in range(a_ref.shape[0]):
        out[x] = interior(g_ref[x], w_ref[x], a_ref[x], c_ref[x], 1)


def z_ends(edges, low, high, lanes):
    shift = lambda value, by: pltpu.roll(value, by % lanes, 1)
    w, a, c = edges
    _, place = edge_lanes(w.shape, lanes)
    low = [shift(low, -v) if v else low for v in range(6)]
    first, second = low_end(low, w, shift(w, -1), a, shift(a, -1), c)
    high = [shift(high, -v) if v else high for v in range(5)]
    last, before = high_end(
        high, shift(w, 2), shift(w, 1), shift(a, 2), shift(a, 1), shift(c, 2), shift(c, 1)
    )
    ends = jnp.where(place == 0, first, jnp.where(place == 1, shift(second, 1), 0.0))
    return jnp.where(
        place == slot - 1, shift(last, -1), jnp.where(place == slot - 2, shift(before, -2), ends)
    )


def spread(ends, x, r, planes, lanes):
    move = slot * (x + planes * r)
    return pltpu.roll(ends, lanes - move, 1) if move else ends


def z_sweep(sizes, partial, edges, opened, ay, cy, ax, cx, *rest):
    n_in = colours(sizes, 2)
    messages, (ends_ref, *out) = [m[...] for m in rest[:n_in]], rest[n_in:]
    planes, rows, lanes = ay.shape
    per = fold(planes, rows, lanes)
    step = rows // per
    low, high = received(sizes, 2, messages, edges[0])
    ends = z_ends([edges[n] for n in range(3)], low, high, lanes)
    ends_ref[...] = ends
    if not out:
        return
    at = lax.broadcasted_iota(jnp.int32, (8, lanes), 1)
    near = (at < 2) | (at >= lanes - 2)
    tile = lax.broadcasted_iota(jnp.int32, (8, lanes), 0)
    pick = lambda *tiles: jnp.where(tile < 2, tiles[0], jnp.where(tile < 4, tiles[1], tiles[2]))
    for x in range(planes):
        ws = []
        for rim, group, r in ((slice(0, 8), ends[:8], 0), (slice(rows - 8, rows), ends[step - 8 :], per - 1)):
            g = partial[x, rim] + jnp.where(near, spread(group, x, r, planes, lanes), 0.0)
            ws.append(opened[x, rim].astype(jnp.float32) * g)
        up = pick(
            *(
                pltpu.roll(field, by, 0)
                for field, by in ((ws[1], 2), (ay[x, rows - 8 :], 4), (cy[x, rows - 8 :], 6))
            )
        )
        down = pick(ws[0], pltpu.roll(ay[x, :8], 2, 0), pltpu.roll(cy[x, :8], 4, 0))
        for ref, message in zip(out, to_send(sizes, 1, up, down)):
            ref[x] = message


def x_products(w, cx):
    planes = len(w)
    back = (w[-1] - w[-2]) * jnp.minimum(cx[planes - 2], 0.0)
    forth = (w[1] - w[0]) * jnp.maximum(cx[0], 0.0)
    return (w[-1], w[0]), (back, forth)


def y_inner(sizes, partial_z, ends_ref, opened, ay, cy, ax, cx, partial, w_rims, *out):
    planes, rows, lanes = ay.shape
    ends = ends_ref[...]
    at = lax.broadcasted_iota(jnp.int32, (rows, lanes), 1)
    near = (at < 2) | (at >= lanes - 2)
    tile = lax.broadcasted_iota(jnp.int32, (8, lanes), 0)
    per = fold(planes, rows, lanes)
    ws = []
    for x in range(planes):
        mask = opened[x].astype(jnp.float32)
        parts = jnp.concatenate([spread(ends, x, r, planes, lanes) for r in range(per)], axis=0)
        g = partial_z[x] + jnp.where(near, parts, 0.0)
        w = mask * g
        w_rims[x] = jnp.where(tile < 4, w[:8], w[rows - 8 :])
        g = interior(g, w, ay[x], cy[x], 0)
        partial[x] = g
        ws.append(mask * g)
    pairs = (
        *x_products(ws, cx),
        (ax[planes - 2], ax[0]),
        (ax[planes - 1], ax[1]),
        (cx[planes - 1], cx[0]),
    )
    for v, (up, down) in enumerate(pairs):
        for ref, message in zip(out, to_send(sizes, 0, up, down)):
            ref[v] = message


def y_sweep(sizes, partial, w_rims, opened, ay, cy, cx, *rest):
    n_in = colours(sizes, 1)
    messages, (g_ref, *out) = rest[:n_in], rest[n_in:]
    planes, rows, lanes = ay.shape
    tile = lax.broadcasted_iota(jnp.int32, (8, lanes), 0)
    ws = []
    for x in range(planes):
        low, high = received(sizes, 1, [m[x] for m in messages], ay[x, :8])
        row = lambda ref, n: ref[x, n : n + 1]
        first, second = low_end(
            [low[v : v + 1] for v in range(6)],
            *(row(ref, n) for ref, n in ((w_rims, 0), (w_rims, 1), (ay, 0), (ay, 1), (cy, 0))),
        )
        last, before = high_end(
            [high[v : v + 1] for v in range(5)],
            row(w_rims, 6),
            row(w_rims, 7),
            *(row(ref, n) for ref in (ay, cy) for n in (rows - 2, rows - 1)),
        )
        top = partial[x, :8] + jnp.where(tile == 0, first, jnp.where(tile == 1, second, 0.0))
        bottom = partial[x, rows - 8 :] + jnp.where(
            tile == 7, last, jnp.where(tile == 6, before, 0.0)
        )
        g_ref[x, :8] = top
        g_ref[x, 8 : rows - 8] = partial[x, 8 : rows - 8]
        g_ref[x, rows - 8 :] = bottom
        mask = jnp.where(tile < 4, opened[x, :8], opened[x, rows - 8 :]).astype(jnp.float32)
        ws.append(mask * jnp.where(tile < 4, top, bottom))
    if out:
        c = [jnp.where(tile < 4, cx[x, :8], cx[x, rows - 8 :]) for x in range(planes)]
        for v, (up, down) in enumerate(x_products(ws, c)):
            for ref, message in zip(out, to_send(sizes, 0, up, down)):
                ref[v] = message


def x_sweep(sizes, g, opened, ax, cx, *rest):
    n_in = colours(sizes, 0)
    early, late, (out, stage, sems) = rest[:n_in], rest[n_in : 2 * n_in], rest[2 * n_in :]
    planes, rows, lanes = ax.shape
    tile = lax.broadcasted_iota(jnp.int32, (8, lanes), 0)

    def whole(n, v):
        if v > 1:
            return early[n][v]
        top = jnp.where(tile < 2, late[n][v], early[n][v, :8])
        bottom = jnp.where(tile >= 6, late[n][v], early[n][v, rows - 8 :])
        return jnp.concatenate([top, early[n][v, 8 : rows - 8], bottom], axis=0)

    (w_low, w_high), (b_low, f_high), (f0, h0), (f1, h1), (c_low, _) = (
        received(sizes, 0, [whole(n, v) for n in range(n_in)], ax[0]) for v in range(5)
    )
    last = planes - 1
    w = [opened[x].astype(jnp.float32) * g[x] for x in range(planes)]
    a = [f1, *(ax[x] for x in range(planes)), h0]
    c = [c_low, *(cx[x] for x in range(planes))]
    _, bent = bend(f1, a[1] - f0)
    r = [((w[0] - w_low) * jnp.maximum(c_low, 0.0) - b_low) * bent]
    own, copies = [], []

    def leave(x):
        stage[x] = own[x] + (r[x] - r[x + 2])
        copies.append(pltpu.make_async_copy(stage.at[x], out.at[x], sems.at[x]))
        copies[-1].start()

    for x in range(planes):
        t, bent = bend(a[x + 1], a[x + 2] - a[x])
        forth = ((w[x + 1] if x < last else w_high) - w[x]) * jnp.maximum(c[x + 1], 0.0)
        back = (w[x] - (w[x - 1] if x else w_low)) * jnp.minimum(c[x], 0.0)
        apart = forth - back
        r.append(apart * bent)
        own.append(
            g[x] + w[x] * (c[x + 1] - c[x]) + (forth + back) + apart * ((0.5 - a[x + 1]) * t)
        )
        if x:
            leave(x - 1)
    _, bent = bend(h0, h1 - a[planes])
    r.append((f_high - (w_high - w[last]) * jnp.minimum(c[planes], 0.0)) * bent)
    leave(last)
    for copy in copies:
        copy.wait()


def call(body, out, *args, name, loads=(), scratch=(), flops=0, target=pltpu.VMEM):
    shapes = [jax.ShapeDtypeStruct(o, jnp.float32) if isinstance(o, tuple) else o for o in out]
    loads = [pltpu.with_memory_space_constraint(v, pltpu.HBM) for v in loads]
    return pl.pallas_call(
        body,
        out_shape=shapes,
        in_specs=[pl.BlockSpec(memory_space=pltpu.VMEM)] * len(args)
        + [pl.BlockSpec(memory_space=pltpu.HBM)] * len(loads),
        out_specs=[pl.BlockSpec(memory_space=target)] * len(shapes),
        scratch_shapes=scratch,
        compiler_params=pltpu.CompilerParams(vmem_limit_bytes=8 * 2**20),
        cost_estimate=pl.CostEstimate(flops=flops, bytes_accessed=2**20, transcendentals=0),
        name=name,
    )(*args, *loads)


def per_device(sizes, cot, ax, ay, az, cx, cy, cz, opened):
    x_rounds, y_rounds, z_rounds = (pair_rounds(sizes, d) for d in range(3))
    early_rounds = pair_rounds(sizes, 0, 1)
    x_rounds = pair_rounds(sizes, 0, 0)
    block = az.shape
    planes, rows, lanes = block
    swap = lambda value, perm: lax.ppermute(value, AXES, perm)
    packed = (rows // fold(planes, rows, lanes), lanes)
    dma = pltpu.SemaphoreType.DMA
    cot, opened, az, cz, w, edges, *z_out = call(
        functools.partial(z_pack, sizes, planes, rows, lanes),
        [block, jax.ShapeDtypeStruct(block, jnp.int32), block, block, block, (3, *packed)]
        + [packed] * len(z_rounds),
        loads=(cot, opened, az, cz),
        name="z_pack", scratch=[dma((4, planes))],
    )
    z_in = [swap(m, p) for m, p in zip(z_out, z_rounds)]
    (partial,) = call(z_inner, [block], cot, w, az, cz, name="z_inner")
    ends, *y_out = call(
        functools.partial(z_sweep, sizes),
        [packed] + [(planes, 8, lanes)] * len(y_rounds),
        partial, edges, opened, ay, cy, ax, cx, *z_in,
        name="z_sweep",
    )
    y_in = [swap(m, p) for m, p in zip(y_out, y_rounds)]
    partial, w_rims, *x_out = call(
        functools.partial(y_inner, sizes),
        [block, (planes, 8, lanes)] + [(5, rows, lanes)] * len(x_rounds),
        partial, ends, opened, ay, cy, ax, cx,
        name="y_inner",
    )
    x_early = [swap(m, p) for m, p in zip(x_out, early_rounds)]
    g, *x_out = call(
        functools.partial(y_sweep, sizes),
        [block] + [(2, 8, lanes)] * len(x_rounds),
        partial, w_rims, opened, ay, cy, cx, *y_in,
        name="y_sweep", flops=10**10,
    )
    x_late = [swap(m, p) for m, p in zip(x_out, x_rounds)]
    (out,) = call(
        functools.partial(x_sweep, sizes), [block], g, opened, ax, cx, *x_early, *x_late,
        target=pltpu.HBM, name="x_sweep",
        scratch=[pltpu.VMEM(block, jnp.float32), dma((planes,))],
    )
    return out


def solution(mesh):
    sizes = tuple(mesh.shape[axis] for axis in AXES)
    placed = P(*AXES)
    return jax.shard_map(
        functools.partial(per_device, sizes),
        mesh=mesh,
        in_specs=(placed,) * 8,
        out_specs=placed,
        check_vma=False,
    )
```

```python
import functools
import itertools

import jax
import jax.numpy as jnp
from jax import lax
from jax.experimental import pallas as pl
from jax.experimental.pallas import tpu as pltpu
from jax.sharding import PartitionSpec as P

sharpness = 3.5
slot = 8
AXES = ("gx", "gy", "gz")


def colours(sizes, along):
    return min(sizes[along] - 1, 3 if along == 2 else 2)


def turn_of(face, along, n):
    return (face + (1 if along == 0 else 0)) % n


def pair_rounds(sizes, along, aside=0):
    n = colours(sizes, along)

    def partner(at, turn):
        at = list(at)
        i = at[along]
        if turn_of(i, along, n) == turn and i + 1 < sizes[along]:
            at[along] += 1
        elif i > 0 and turn_of(i - 1, along, n) == turn:
            at[along] -= 1
        elif aside == along:
            at[along] = sizes[along] - 1 - i
        elif sizes[aside] % 2 == 0:
            at[aside] ^= 1
        return at

    places = list(itertools.product(*(range(size) for size in sizes)))
    flat = lambda at: (at[0] * sizes[1] + at[1]) * sizes[2] + at[2]
    return [[(flat(at), flat(partner(at, turn))) for at in places] for turn in range(n)]


def to_send(sizes, along, up, down):
    n, at = colours(sizes, along), lax.axis_index(AXES[along])
    if n <= 1:
        return [jnp.where(at == 0, up, down)] * n
    mine = turn_of(at, along, n)
    return [jnp.where((mine == turn) & (at < sizes[along] - 1), up, down) for turn in range(n)]


def received(sizes, along, messages, like):
    n, at = colours(sizes, along), lax.axis_index(AXES[along])
    if n == 0:
        return jnp.zeros_like(like), jnp.zeros_like(like)
    low = high = messages[0]
    for turn in range(1, n):
        low = jnp.where(turn_of(at + n - 1, along, n) == turn, messages[turn], low)
        high = jnp.where(turn_of(at, along, n) == turn, messages[turn], high)
    return jnp.where(at > 0, low, 0.0), jnp.where(at < sizes[along] - 1, high, 0.0)


def bend(a, difference):
    t = jnp.tanh(sharpness * difference)
    return t, 0.5 * sharpness * a * (1.0 - a) * (1.0 - t * t)


def low_end(low, w0, w1, a0, a1, c0):
    w_far, w_low, a_far, a_low, c_far, c_low = low
    _, bent = bend(a_low, a0 - a_far)
    across = w0 - w_low
    r_low = (across * jnp.maximum(c_low, 0.0) - (w_low - w_far) * jnp.minimum(c_far, 0.0)) * bent
    forth = (w1 - w0) * jnp.maximum(c0, 0.0)
    back = across * jnp.minimum(c_low, 0.0)
    t, bent = bend(a0, a1 - a_low)
    first = w0 * (c0 - c_low) + (forth + back) + (forth - back) * ((0.5 - a0) * t) + r_low
    return first, (forth - back) * bent


def high_end(high, w0, w1, a0, a1, c0, c1):
    w_high, w_far, a_high, a_far, c_high = high
    _, bent = bend(a_high, a_far - a1)
    across = w_high - w1
    r_high = ((w_far - w_high) * jnp.maximum(c_high, 0.0) - across * jnp.minimum(c1, 0.0)) * bent
    forth = across * jnp.maximum(c1, 0.0)
    back = (w1 - w0) * jnp.minimum(c0, 0.0)
    t, bent = bend(a1, a_high - a0)
    last = w1 * (c1 - c0) + (forth + back) + (forth - back) * ((0.5 - a1) * t) - r_high
    return last, (back - forth) * bent


def factors(a, c, dim):
    length = a.shape[dim]
    at = lax.broadcasted_iota(jnp.int32, a.shape, dim)
    inside = (at > 0) & (at < length - 1)
    below = pltpu.roll(c, 1, dim)
    t, bent = bend(a, pltpu.roll(a, length - 1, dim) - pltpu.roll(a, 1, dim))
    return (
        jnp.where(inside, c - below, 0.0),
        jnp.where(inside, jnp.maximum(c, 0.0), 0.0),
        jnp.where(inside, jnp.minimum(below, 0.0), 0.0),
        (0.5 - a) * t,
        bent,
    )


def interior(g, w, parts, dim):
    rise, ahead, behind, lean, bent = parts
    length = w.shape[dim]
    prev = lambda value: pltpu.roll(value, 1, dim)
    after = lambda value: pltpu.roll(value, length - 1, dim)
    forth = (after(w) - w) * ahead
    back = (w - prev(w)) * behind
    apart = forth - back
    r = apart * bent
    return g + (w * rise + (forth + back) + apart * lean) + (prev(r) - after(r))


def fold(planes, rows, lanes):
    per = lanes // (slot * planes)
    return per if per >= 1 and rows % (8 * per) == 0 else 1


def edge_lanes(shape, lanes):
    at = lax.broadcasted_iota(jnp.int32, shape, 1)
    return at, lax.rem(at, slot)


def z_pack(sizes, planes, rows, lanes, *refs):
    sources, targets, (w_ref, edge_ref, *out, sems) = refs[:4], refs[4:8], refs[8:]
    copies = [
        [
            pltpu.make_async_copy(src.at[x], dst.at[x], sems.at[n, x])
            for n, (src, dst) in enumerate(zip(sources, targets))
        ]
        for x in range(planes)
    ]
    for copy in itertools.chain(*copies):
        copy.start()
    cot, opened, a_ref, c_ref = targets
    per = fold(planes, rows, lanes)
    step = rows // per
    at, place = edge_lanes((rows, lanes), lanes)
    near = (at < 2) | (at >= lanes - 2)
    totals = [None] * 3
    for x in range(planes):
        for copy in itertools.chain(*({0: copies[:2], 2: copies[2:]}.get(x, []))):
            copy.wait()
        w = cot[x] * opened[x].astype(jnp.float32)
        w_ref[x] = w
        for n, field in enumerate((w, a_ref[x], c_ref[x])):
            field = jnp.where(near, field, 0.0)
            for r in range(per):
                move = slot * (x + planes * r)
                part = field[r * step : (r + 1) * step]
                part = pltpu.roll(part, move, 1) if move else part
                totals[n] = part if totals[n] is None else totals[n] + part
    for n in range(3):
        edge_ref[n] = totals[n]
    _, place = edge_lanes((step, lanes), lanes)
    ends = [jnp.where(place >= slot - 2, total, 0.0) for total in totals]
    starts = [jnp.where(place < 2, total, 0.0) for total in totals]
    up = sum(pltpu.roll(end, 2 + 2 * n, 1) for n, end in enumerate(ends))
    down = sum(pltpu.roll(start, 2 * n, 1) if n else start for n, start in enumerate(starts))
    for ref, message in zip(out, to_send(sizes, 2, up, down)):
        ref[...] = message


def z_inner(g_ref, w_ref, a_ref, c_ref, out):
    for x in range(a_ref.shape[0]):
        out[x] = interior(g_ref[x], w_ref[x], factors(a_ref[x], c_ref[x], 1), 1)


def y_factors(ay, cy, *out):
    for x in range(ay.shape[0]):
        for ref, part in zip(out, factors(ay[x], cy[x], 0)):
            ref[x] = part


def z_ends(edges, low, high, lanes):
    shift = lambda value, by: pltpu.roll(value, by % lanes, 1)
    w, a, c = edges
    _, place = edge_lanes(w.shape, lanes)
    low = [shift(low, -v) if v else low for v in range(6)]
    first, second = low_end(low, w, shift(w, -1), a, shift(a, -1), c)
    high = [shift(high, -v) if v else high for v in range(5)]
    last, before = high_end(
        high, shift(w, 2), shift(w, 1), shift(a, 2), shift(a, 1), shift(c, 2), shift(c, 1)
    )
    ends = jnp.where(place == 0, first, jnp.where(place == 1, shift(second, 1), 0.0))
    return jnp.where(
        place == slot - 1, shift(last, -1), jnp.where(place == slot - 2, shift(before, -2), ends)
    )


def spread(ends, x, r, planes, lanes):
    move = slot * (x + planes * r)
    return pltpu.roll(ends, lanes - move, 1) if move else ends


def z_sweep(sizes, partial, edges, opened, ay, cy, ax, cx, _, *rest):
    n_in = colours(sizes, 2)
    messages, (ends_ref, *out) = [m[...] for m in rest[:n_in]], rest[n_in:]
    planes, rows, lanes = ay.shape
    per = fold(planes, rows, lanes)
    step = rows // per
    low, high = received(sizes, 2, messages, edges[0])
    ends = z_ends([edges[n] for n in range(3)], low, high, lanes)
    ends_ref[...] = ends
    if not out:
        return
    at = lax.broadcasted_iota(jnp.int32, (8, lanes), 1)
    near = (at < 2) | (at >= lanes - 2)
    tile = lax.broadcasted_iota(jnp.int32, (8, lanes), 0)
    pick = lambda *tiles: jnp.where(tile < 2, tiles[0], jnp.where(tile < 4, tiles[1], tiles[2]))
    for x in range(planes):
        ws = []
        for rim, group, r in ((slice(0, 8), ends[:8], 0), (slice(rows - 8, rows), ends[step - 8 :], per - 1)):
            g = partial[x, rim] + jnp.where(near, spread(group, x, r, planes, lanes), 0.0)
            ws.append(opened[x, rim].astype(jnp.float32) * g)
        up = pick(
            *(
                pltpu.roll(field, by, 0)
                for field, by in ((ws[1], 2), (ay[x, rows - 8 :], 4), (cy[x, rows - 8 :], 6))
            )
        )
        down = pick(ws[0], pltpu.roll(ay[x, :8], 2, 0), pltpu.roll(cy[x, :8], 4, 0))
        for ref, message in zip(out, to_send(sizes, 1, up, down)):
            ref[x] = message


def x_products(w, cx):
    planes = len(w)
    back = (w[-1] - w[-2]) * jnp.minimum(cx[planes - 2], 0.0)
    forth = (w[1] - w[0]) * jnp.maximum(cx[0], 0.0)
    return (w[-1], w[0]), (back, forth)


def y_inner(sizes, partial_z, ends_ref, opened, ax, cx, *rest):
    parts_y, (partial, w_rims, *out) = rest[:5], rest[5:]
    planes, rows, lanes = ax.shape
    ends = ends_ref[...]
    at = lax.broadcasted_iota(jnp.int32, (rows, lanes), 1)
    near = (at < 2) | (at >= lanes - 2)
    tile = lax.broadcasted_iota(jnp.int32, (8, lanes), 0)
    per = fold(planes, rows, lanes)
    ws = []
    for x in range(planes):
        mask = opened[x].astype(jnp.float32)
        parts = jnp.concatenate([spread(ends, x, r, planes, lanes) for r in range(per)], axis=0)
        g = partial_z[x] + jnp.where(near, parts, 0.0)
        w = mask * g
        w_rims[x] = jnp.where(tile < 4, w[:8], w[rows - 8 :])
        g = interior(g, w, [part[x] for part in parts_y], 0)
        partial[x] = g
        ws.append(mask * g)
    pairs = (
        *x_products(ws, cx),
        (ax[planes - 2], ax[0]),
        (ax[planes - 1], ax[1]),
    )
    for v, (up, down) in enumerate(pairs):
        for ref, message in zip(out, to_send(sizes, 0, up, down)):
            ref[v * rows : (v + 1) * rows] = message
    half = slice(0, rows // 2)
    for ref, message in zip(out, to_send(sizes, 0, cx[planes - 1, half], cx[0, half])):
        ref[4 * rows :] = message


def y_sweep(sizes, partial, w_rims, opened, ay, cy, cx, *rest):
    n_in = colours(sizes, 1)
    messages, (g_ref, *out) = rest[:n_in], rest[n_in:]
    planes, rows, lanes = ay.shape
    tile = lax.broadcasted_iota(jnp.int32, (8, lanes), 0)
    ws = []
    for x in range(planes):
        low, high = received(sizes, 1, [m[x] for m in messages], ay[x, :8])
        row = lambda ref, n: ref[x, n : n + 1]
        first, second = low_end(
            [low[v : v + 1] for v in range(6)],
            *(row(ref, n) for ref, n in ((w_rims, 0), (w_rims, 1), (ay, 0), (ay, 1), (cy, 0))),
        )
        last, before = high_end(
            [high[v : v + 1] for v in range(5)],
            row(w_rims, 6),
            row(w_rims, 7),
            *(row(ref, n) for ref in (ay, cy) for n in (rows - 2, rows - 1)),
        )
        top = partial[x, :8] + jnp.where(tile == 0, first, jnp.where(tile == 1, second, 0.0))
        bottom = partial[x, rows - 8 :] + jnp.where(
            tile == 7, last, jnp.where(tile == 6, before, 0.0)
        )
        g_ref[x, :8] = top
        g_ref[x, 8 : rows - 8] = partial[x, 8 : rows - 8]
        g_ref[x, rows - 8 :] = bottom
        mask = jnp.where(tile < 4, opened[x, :8], opened[x, rows - 8 :]).astype(jnp.float32)
        ws.append(mask * jnp.where(tile < 4, top, bottom))
    if out:
        c = [jnp.where(tile < 4, cx[x, :8], cx[x, rows - 8 :]) for x in range(planes)]
        for v, (up, down) in enumerate(x_products(ws, c)):
            for ref, message in zip(out, to_send(sizes, 0, up, down)):
                ref[8 * v : 8 * v + 8] = message
        half = slice(rows // 2, rows)
        for ref, message in zip(out, to_send(sizes, 0, cx[planes - 1, half], cx[0, half])):
            ref[16:] = message


def x_inner(g_ref, opened, ax, cx, ready, own_ref, r_ref):
    planes = ax.shape[0]
    last = planes - 1
    w = [opened[x].astype(jnp.float32) * g_ref[x] for x in range(planes)]
    ready[0], ready[1] = w[0], w[last]
    ready[2] = (w[1] - w[0]) * jnp.maximum(cx[0], 0.0)
    ready[3] = (w[last] - w[last - 1]) * jnp.minimum(cx[last - 1], 0.0)
    for x in range(1, last):
        t, bent = bend(ax[x], ax[x + 1] - ax[x - 1])
        forth = (w[x + 1] - w[x]) * jnp.maximum(cx[x], 0.0)
        back = (w[x] - w[x - 1]) * jnp.minimum(cx[x - 1], 0.0)
        apart = forth - back
        r_ref[x - 1] = apart * bent
        own_ref[x - 1] = (
            g_ref[x] + w[x] * (cx[x] - cx[x - 1]) + (forth + back) + apart * ((0.5 - ax[x]) * t)
        )


def x_sweep(sizes, g_ref, ax, cx, ready, own_ref, r_ref, *rest):
    n_in = colours(sizes, 0)
    early, late, (out, stage, sems) = rest[:n_in], rest[n_in : 2 * n_in], rest[2 * n_in :]
    planes, rows, lanes = ax.shape
    last = planes - 1
    tile = lax.broadcasted_iota(jnp.int32, (8, lanes), 0)

    def whole(n, v):
        if v == 4:
            return jnp.concatenate([early[n][4 * rows :], late[n][16:]], axis=0)
        value = early[n][v * rows : (v + 1) * rows]
        if v > 1:
            return value
        ends = late[n][8 * v : 8 * v + 8]
        top = jnp.where(tile < 2, ends, value[:8])
        bottom = jnp.where(tile >= 6, ends, value[rows - 8 :])
        return jnp.concatenate([top, value[8 : rows - 8], bottom], axis=0)

    (w_low, w_high), (b_low, f_high), (f0, h0), (f1, h1), (c_low, _) = (
        received(sizes, 0, [whole(n, v) for n in range(n_in)], ax[0]) for v in range(5)
    )
    copies = []

    def leave(x, value):
        stage[x] = value
        copies.append(pltpu.make_async_copy(stage.at[x], out.at[x], sems.at[x]))
        copies[-1].start()

    def outer(x, w, a_next, forth, back, c_low):
        t, bent = bend(ax[x], a_next)
        apart = forth - back
        own = g_ref[x] + w * (cx[x] - c_low) + (forth + back) + apart * ((0.5 - ax[x]) * t)
        return own, apart * bent

    w_first, w_last = ready[0], ready[1]
    across = w_first - w_low
    own_first, r_first = outer(
        0, w_first, ax[1] - f1, ready[2], across * jnp.minimum(c_low, 0.0), c_low
    )
    _, bent = bend(f1, ax[0] - f0)
    r_low = (across * jnp.maximum(c_low, 0.0) - b_low) * bent
    across = w_high - w_last
    own_last, r_last = outer(
        last, w_last, h0 - ax[last - 1], across * jnp.maximum(cx[last], 0.0), ready[3], cx[last - 1]
    )
    _, bent = bend(h0, h1 - ax[last])
    r_high = (f_high - across * jnp.minimum(cx[last], 0.0)) * bent
    r = [r_low, r_first, *(r_ref[x] for x in range(last - 1)), r_last, r_high]
    for x in range(planes):
        own = own_first if x == 0 else own_last if x == last else own_ref[x - 1]
        leave(x, own + (r[x] - r[x + 2]))
    for copy in copies:
        copy.wait()


def call(body, out, *args, name, loads=(), scratch=(), flops=0, target=pltpu.VMEM):
    shapes = [jax.ShapeDtypeStruct(o, jnp.float32) if isinstance(o, tuple) else o for o in out]
    loads = [pltpu.with_memory_space_constraint(v, pltpu.HBM) for v in loads]
    return pl.pallas_call(
        body,
        out_shape=shapes,
        in_specs=[pl.BlockSpec(memory_space=pltpu.VMEM)] * len(args)
        + [pl.BlockSpec(memory_space=pltpu.HBM)] * len(loads),
        out_specs=[pl.BlockSpec(memory_space=target)] * len(shapes),
        scratch_shapes=scratch,
        compiler_params=pltpu.CompilerParams(vmem_limit_bytes=8 * 2**20),
        cost_estimate=pl.CostEstimate(flops=flops, bytes_accessed=2**20, transcendentals=0),
        name=name,
    )(*args, *loads)


def per_device(sizes, cot, ax, ay, az, cx, cy, cz, opened):
    x_rounds, y_rounds, z_rounds = (pair_rounds(sizes, d) for d in range(3))
    early_rounds = pair_rounds(sizes, 0, 1)
    x_rounds = pair_rounds(sizes, 0, 0)
    block = az.shape
    planes, rows, lanes = block
    swap = lambda value, perm: lax.ppermute(value, AXES, perm)
    packed = (rows // fold(planes, rows, lanes), lanes)
    dma = pltpu.SemaphoreType.DMA
    cot, opened, az, cz, w, edges, *z_out = call(
        functools.partial(z_pack, sizes, planes, rows, lanes),
        [block, jax.ShapeDtypeStruct(block, jnp.int32), block, block, block, (3, *packed)]
        + [packed] * len(z_rounds),
        loads=(cot, opened, az, cz),
        name="z_pack", scratch=[dma((4, planes))],
    )
    z_in = [swap(m, p) for m, p in zip(z_out, z_rounds)]
    (partial,) = call(z_inner, [block], cot, w, az, cz, name="z_inner")
    parts_y = call(y_factors, [block] * 5, ay, cy, name="y_factors")
    ends, *y_out = call(
        functools.partial(z_sweep, sizes),
        [packed] + [(planes, 8, lanes)] * len(y_rounds),
        partial, edges, opened, ay, cy, ax, cx, parts_y[0], *z_in,
        name="z_sweep",
    )
    y_in = [swap(m, p) for m, p in zip(y_out, y_rounds)]
    partial, w_rims, *x_out = call(
        functools.partial(y_inner, sizes),
        [block, (planes, 8, lanes)] + [(4 * rows + rows // 2, lanes)] * len(x_rounds),
        partial, ends, opened, ax, cx, *parts_y,
        name="y_inner",
    )
    x_early = [swap(m, p) for m, p in zip(x_out, early_rounds)]
    g, *x_out = call(
        functools.partial(y_sweep, sizes),
        [block] + [(16 + rows // 2, lanes)] * len(x_rounds),
        partial, w_rims, opened, ay, cy, cx, *y_in,
        name="y_sweep", flops=10**10,
    )
    x_late = [swap(m, p) for m, p in zip(x_out, x_rounds)]
    ready = call(
        x_inner, [(4, rows, lanes)] + [(planes - 2, rows, lanes)] * 2, g, opened, ax, cx, name="x_inner"
    )
    (out,) = call(
        functools.partial(x_sweep, sizes), [block], g, ax, cx, *ready, *x_early, *x_late,
        target=pltpu.HBM, name="x_sweep",
        scratch=[pltpu.VMEM(block, jnp.float32), dma((planes,))],
    )
    return out


def solution(mesh):
    sizes = tuple(mesh.shape[axis] for axis in AXES)
    placed = P(*AXES)
    return jax.shard_map(
        functools.partial(per_device, sizes),
        mesh=mesh,
        in_specs=(placed,) * 8,
        out_specs=placed,
        check_vma=False,
    )
```

```python
import functools
import itertools

import jax
import jax.numpy as jnp
from jax import lax
from jax.experimental import pallas as pl
from jax.experimental.pallas import tpu as pltpu
from jax.sharding import PartitionSpec as P

sharpness = 3.5
slot = 8
AXES = ("gx", "gy", "gz")


def colours(sizes, along):
    return min(sizes[along] - 1, 3 if along == 2 else 2)


def turn_of(face, along, n):
    return (face + (1 if along == 0 else 0)) % n


def pair_rounds(sizes, along, aside=0):
    n = colours(sizes, along)

    def partner(at, turn):
        at = list(at)
        i = at[along]
        if turn_of(i, along, n) == turn and i + 1 < sizes[along]:
            at[along] += 1
        elif i > 0 and turn_of(i - 1, along, n) == turn:
            at[along] -= 1
        elif aside == along:
            at[along] = sizes[along] - 1 - i
        elif sizes[aside] % 2 == 0:
            at[aside] ^= 1
        return at

    places = list(itertools.product(*(range(size) for size in sizes)))
    flat = lambda at: (at[0] * sizes[1] + at[1]) * sizes[2] + at[2]
    return [[(flat(at), flat(partner(at, turn))) for at in places] for turn in range(n)]


def to_send(sizes, along, up, down):
    n, at = colours(sizes, along), lax.axis_index(AXES[along])
    if n <= 1:
        return [jnp.where(at == 0, up, down)] * n
    mine = turn_of(at, along, n)
    return [jnp.where((mine == turn) & (at < sizes[along] - 1), up, down) for turn in range(n)]


def received(sizes, along, messages, like):
    n, at = colours(sizes, along), lax.axis_index(AXES[along])
    if n == 0:
        return jnp.zeros_like(like), jnp.zeros_like(like)
    low = high = messages[0]
    for turn in range(1, n):
        low = jnp.where(turn_of(at + n - 1, along, n) == turn, messages[turn], low)
        high = jnp.where(turn_of(at, along, n) == turn, messages[turn], high)
    return jnp.where(at > 0, low, 0.0), jnp.where(at < sizes[along] - 1, high, 0.0)


def bend(a, difference):
    t = jnp.tanh(sharpness * difference)
    return t, 0.5 * sharpness * a * (1.0 - a) * (1.0 - t * t)


def low_end(low, w0, w1, a0, a1, c0):
    w_far, w_low, a_far, a_low, c_far, c_low = low
    _, bent = bend(a_low, a0 - a_far)
    across = w0 - w_low
    r_low = (across * jnp.maximum(c_low, 0.0) - (w_low - w_far) * jnp.minimum(c_far, 0.0)) * bent
    forth = (w1 - w0) * jnp.maximum(c0, 0.0)
    back = across * jnp.minimum(c_low, 0.0)
    t, bent = bend(a0, a1 - a_low)
    first = w0 * (c0 - c_low) + (forth + back) + (forth - back) * ((0.5 - a0) * t) + r_low
    return first, (forth - back) * bent


def high_end(high, w0, w1, a0, a1, c0, c1):
    w_high, w_far, a_high, a_far, c_high = high
    _, bent = bend(a_high, a_far - a1)
    across = w_high - w1
    r_high = ((w_far - w_high) * jnp.maximum(c_high, 0.0) - across * jnp.minimum(c1, 0.0)) * bent
    forth = across * jnp.maximum(c1, 0.0)
    back = (w1 - w0) * jnp.minimum(c0, 0.0)
    t, bent = bend(a1, a_high - a0)
    last = w1 * (c1 - c0) + (forth + back) + (forth - back) * ((0.5 - a1) * t) - r_high
    return last, (back - forth) * bent


def factors(a, c, dim):
    length = a.shape[dim]
    at = lax.broadcasted_iota(jnp.int32, a.shape, dim)
    inside = (at > 0) & (at < length - 1)
    below = pltpu.roll(c, 1, dim)
    t, bent = bend(a, pltpu.roll(a, length - 1, dim) - pltpu.roll(a, 1, dim))
    return (
        jnp.where(inside, c - below, 0.0),
        jnp.where(inside, jnp.maximum(c, 0.0), 0.0),
        jnp.where(inside, jnp.minimum(below, 0.0), 0.0),
        (0.5 - a) * t,
        bent,
    )


def interior(g, w, parts, dim):
    rise, ahead, behind, lean, bent = parts
    length = w.shape[dim]
    prev = lambda value: pltpu.roll(value, 1, dim)
    after = lambda value: pltpu.roll(value, length - 1, dim)
    forth = (after(w) - w) * ahead
    back = (w - prev(w)) * behind
    apart = forth - back
    r = apart * bent
    return g + (w * rise + (forth + back) + apart * lean) + (prev(r) - after(r))


def fold(planes, rows, lanes):
    per = lanes // (slot * planes)
    return per if per >= 1 and rows % (8 * per) == 0 else 1


def edge_lanes(shape, lanes):
    at = lax.broadcasted_iota(jnp.int32, shape, 1)
    return at, lax.rem(at, slot)


def z_pack(sizes, planes, rows, lanes, *refs):
    sources, targets, (w_ref, edge_ref, *out, sems) = refs[:4], refs[4:8], refs[8:]
    copies = [
        [
            pltpu.make_async_copy(src.at[x], dst.at[x], sems.at[n, x])
            for n, (src, dst) in enumerate(zip(sources, targets))
        ]
        for x in range(planes)
    ]
    for copy in itertools.chain(*copies):
        copy.start()
    cot, opened, a_ref, c_ref = targets
    per = fold(planes, rows, lanes)
    step = rows // per
    at, place = edge_lanes((rows, lanes), lanes)
    near = (at < 2) | (at >= lanes - 2)
    totals = [None] * 2
    for x in range(planes):
        for copy in itertools.chain(*({0: copies[:2], 2: copies[2:]}.get(x, []))):
            copy.wait()
        w = cot[x] * opened[x].astype(jnp.float32)
        w_ref[x] = w
        for n, field, lane in ((0, w, 2), (0, a_ref[x], 6), (1, c_ref[x], 4)):
            field = jnp.where(near, field, 0.0)
            for r in range(per):
                part = field[r * step : (r + 1) * step]
                part = pltpu.roll(part, (slot * (x + planes * r) + lane) % lanes, 1)
                totals[n] = part if totals[n] is None else totals[n] + part
    for n in range(2):
        edge_ref[n] = totals[n]
    _, place = edge_lanes((step, lanes), lanes)
    up = jnp.where(lax.rem(place, 4) < 2, totals[0], jnp.where(place < 4, totals[1], 0.0))
    down = jnp.where(lax.rem(place, 4) >= 2, totals[0], jnp.where(place >= 4, totals[1], 0.0))
    for ref, message in zip(out, to_send(sizes, 2, up, down)):
        ref[...] = message


def z_inner(g_ref, w_ref, a_ref, c_ref, out):
    for x in range(a_ref.shape[0]):
        out[x] = interior(g_ref[x], w_ref[x], factors(a_ref[x], c_ref[x], 1), 1)


def y_factors(ay, cy, *out):
    for x in range(ay.shape[0]):
        for ref, part in zip(out, factors(ay[x], cy[x], 0)):
            ref[x] = part


def z_ends(edges, low, high, lanes):
    lane = lambda value, at: pltpu.roll(value, lanes - at, 1) if at else value
    wa, c = edges
    w_far, w_low, c_far, c_low, a_far, a_low = (lane(low, at) for at in range(6))
    first, second = low_end(
        (w_far, w_low, a_far, a_low, c_far, c_low),
        *(lane(wa, at) for at in (2, 3, 6, 7)),
        lane(c, 4),
    )
    w_high, w_far, c_high, a_high, a_far = (lane(high, at) for at in (2, 3, 4, 6, 7))
    last, before = high_end(
        (w_high, w_far, a_high, a_far, c_high),
        *(lane(wa, at) for at in (0, 1, 4, 5)),
        *(lane(c, at) for at in (2, 3)),
    )
    return first, second, last, before


columns = (0, 1, -1, -2)


def spread(ends, x, r, planes, lanes, column=0):
    move = (column - slot * (x + planes * r)) % lanes
    return pltpu.roll(ends, move, 1) if move else ends


def on_columns(at, lanes, values):
    total = 0.0
    for column, value in zip(columns, values):
        total = jnp.where(at == column % lanes, value, total)
    return total


def z_sweep(sizes, partial, edges, opened, ay, cy, ax, cx, _, *rest):
    n_in = colours(sizes, 2)
    messages, (ends_ref, *out) = [m[...] for m in rest[:n_in]], rest[n_in:]
    planes, rows, lanes = ay.shape
    per = fold(planes, rows, lanes)
    step = rows // per
    low, high = received(sizes, 2, messages, edges[0])
    ends = z_ends([edges[0], edges[1]], low, high, lanes)
    _, place = edge_lanes((step, lanes), lanes)
    ends_ref[...] = on_columns(
        place, slot, [spread(end, 0, 0, planes, lanes, column) for end, column in zip(ends, columns)]
    )
    if not out:
        return
    at = lax.broadcasted_iota(jnp.int32, (8, lanes), 1)
    tile = lax.broadcasted_iota(jnp.int32, (8, lanes), 0)
    for x in range(planes):
        ws = []
        for rim, group, r in ((slice(0, 8), slice(0, 8), 0), (slice(rows - 8, rows), slice(step - 8, step), per - 1)):
            added = [
                spread(end[group], x, r, planes, lanes, column) for end, column in zip(ends, columns)
            ]
            g = partial[x, rim] + on_columns(at, lanes, added)
            ws.append(opened[x, rim].astype(jnp.float32) * g)
        a, c = (pltpu.roll(ref[x, rows - 8 :], by, 0) for ref, by in ((ay, 6), (cy, 4)))
        up = jnp.where(tile >= 6, ws[1], jnp.where(tile >= 4, a, c))
        a, c = (pltpu.roll(ref[x, :8], by, 0) for ref, by in ((ay, 2), (cy, 4)))
        down = jnp.where(tile < 2, ws[0], jnp.where(tile < 4, a, c))
        for ref, message in zip(out, to_send(sizes, 1, up, down)):
            ref[x] = message


def x_products(w, cx):
    planes = len(w)
    back = (w[-1] - w[-2]) * jnp.minimum(cx[planes - 2], 0.0)
    forth = (w[1] - w[0]) * jnp.maximum(cx[0], 0.0)
    return (w[-1], w[0]), (back, forth)


def y_inner(sizes, partial_z, ends_ref, opened, ax, cx, *rest):
    parts_y, (partial, w_rims, *out) = rest[:5], rest[5:]
    planes, rows, lanes = ax.shape
    ends = ends_ref[...]
    at = lax.broadcasted_iota(jnp.int32, (rows, lanes), 1)
    near = (at < 2) | (at >= lanes - 2)
    tile = lax.broadcasted_iota(jnp.int32, (8, lanes), 0)
    per = fold(planes, rows, lanes)
    ws = []
    for x in range(planes):
        mask = opened[x].astype(jnp.float32)
        parts = jnp.concatenate([spread(ends, x, r, planes, lanes) for r in range(per)], axis=0)
        g = partial_z[x] + jnp.where(near, parts, 0.0)
        w = mask * g
        w_rims[x] = jnp.where(tile < 4, w[:8], w[rows - 8 :])
        g = interior(g, w, [part[x] for part in parts_y], 0)
        partial[x] = g
        ws.append(mask * g)
    pairs = (
        *x_products(ws, cx),
        (ax[planes - 2], ax[0]),
        (ax[planes - 1], ax[1]),
    )
    for v, (up, down) in enumerate(pairs):
        for ref, message in zip(out, to_send(sizes, 0, up, down)):
            ref[v * rows : (v + 1) * rows] = message
    half = slice(0, rows // 2)
    for ref, message in zip(out, to_send(sizes, 0, cx[planes - 1, half], cx[0, half])):
        ref[4 * rows :] = message


def y_sweep(sizes, partial, w_rims, opened, ay, cy, cx, *rest):
    n_in = colours(sizes, 1)
    messages, (g_ref, *out) = rest[:n_in], rest[n_in:]
    planes, rows, lanes = ay.shape
    tile = lax.broadcasted_iota(jnp.int32, (8, lanes), 0)
    ws = []
    for x in range(planes):
        low, high = received(sizes, 1, [m[x] for m in messages], ay[x, :8])
        row = lambda ref, n: ref[x, n : n + 1]
        first, second = low_end(
            [low[v : v + 1] for v in (6, 7, 4, 5, 2, 3)],
            *(row(ref, n) for ref, n in ((w_rims, 0), (w_rims, 1), (ay, 0), (ay, 1), (cy, 0))),
        )
        last, before = high_end(
            [high[v : v + 1] for v in range(5)],
            row(w_rims, 6),
            row(w_rims, 7),
            *(row(ref, n) for ref in (ay, cy) for n in (rows - 2, rows - 1)),
        )
        top = partial[x, :8] + jnp.where(tile == 0, first, jnp.where(tile == 1, second, 0.0))
        bottom = partial[x, rows - 8 :] + jnp.where(
            tile == 7, last, jnp.where(tile == 6, before, 0.0)
        )
        g_ref[x, :8] = top
        g_ref[x, 8 : rows - 8] = partial[x, 8 : rows - 8]
        g_ref[x, rows - 8 :] = bottom
        mask = jnp.where(tile < 4, opened[x, :8], opened[x, rows - 8 :]).astype(jnp.float32)
        ws.append(mask * jnp.where(tile < 4, top, bottom))
    if out:
        c = [jnp.where(tile < 4, cx[x, :8], cx[x, rows - 8 :]) for x in range(planes)]
        for v, (up, down) in enumerate(x_products(ws, c)):
            for ref, message in zip(out, to_send(sizes, 0, up, down)):
                ref[8 * v : 8 * v + 8] = message
        half = slice(rows // 2, rows)
        for ref, message in zip(out, to_send(sizes, 0, cx[planes - 1, half], cx[0, half])):
            ref[16:] = message


def x_inner(g_ref, opened, ax, cx, ready, own_ref, r_ref):
    planes = ax.shape[0]
    last = planes - 1
    w = [opened[x].astype(jnp.float32) * g_ref[x] for x in range(planes)]
    ready[0], ready[1] = w[0], w[last]
    ready[2] = (w[1] - w[0]) * jnp.maximum(cx[0], 0.0)
    ready[3] = (w[last] - w[last - 1]) * jnp.minimum(cx[last - 1], 0.0)
    for x in range(1, last):
        t, bent = bend(ax[x], ax[x + 1] - ax[x - 1])
        forth = (w[x + 1] - w[x]) * jnp.maximum(cx[x], 0.0)
        back = (w[x] - w[x - 1]) * jnp.minimum(cx[x - 1], 0.0)
        apart = forth - back
        r_ref[x - 1] = apart * bent
        own_ref[x - 1] = (
            g_ref[x] + w[x] * (cx[x] - cx[x - 1]) + (forth + back) + apart * ((0.5 - ax[x]) * t)
        )


def x_sweep(sizes, g_ref, ax, cx, ready, own_ref, r_ref, *rest):
    n_in = colours(sizes, 0)
    early, late, (out, stage, sems) = rest[:n_in], rest[n_in : 2 * n_in], rest[2 * n_in :]
    planes, rows, lanes = ax.shape
    last = planes - 1
    tile = lax.broadcasted_iota(jnp.int32, (8, lanes), 0)

    def whole(n, v):
        if v == 4:
            return jnp.concatenate([early[n][4 * rows :], late[n][16:]], axis=0)
        value = early[n][v * rows : (v + 1) * rows]
        if v > 1:
            return value
        ends = late[n][8 * v : 8 * v + 8]
        top = jnp.where(tile < 2, ends, value[:8])
        bottom = jnp.where(tile >= 6, ends, value[rows - 8 :])
        return jnp.concatenate([top, value[8 : rows - 8], bottom], axis=0)

    (w_low, w_high), (b_low, f_high), (f0, h0), (f1, h1), (c_low, _) = (
        received(sizes, 0, [whole(n, v) for n in range(n_in)], ax[0]) for v in range(5)
    )
    copies = []

    def leave(x, value):
        stage[x] = value
        copies.append(pltpu.make_async_copy(stage.at[x], out.at[x], sems.at[x]))
        copies[-1].start()

    def outer(x, w, a_next, forth, back, c_low):
        t, bent = bend(ax[x], a_next)
        apart = forth - back
        own = g_ref[x] + w * (cx[x] - c_low) + (forth + back) + apart * ((0.5 - ax[x]) * t)
        return own, apart * bent

    w_first, w_last = ready[0], ready[1]
    across = w_first - w_low
    own_first, r_first = outer(
        0, w_first, ax[1] - f1, ready[2], across * jnp.minimum(c_low, 0.0), c_low
    )
    _, bent = bend(f1, ax[0] - f0)
    r_low = (across * jnp.maximum(c_low, 0.0) - b_low) * bent
    across = w_high - w_last
    own_last, r_last = outer(
        last, w_last, h0 - ax[last - 1], across * jnp.maximum(cx[last], 0.0), ready[3], cx[last - 1]
    )
    _, bent = bend(h0, h1 - ax[last])
    r_high = (f_high - across * jnp.minimum(cx[last], 0.0)) * bent
    r = [r_low, r_first, *(r_ref[x] for x in range(last - 1)), r_last, r_high]
    for x in range(planes):
        own = own_first if x == 0 else own_last if x == last else own_ref[x - 1]
        leave(x, own + (r[x] - r[x + 2]))
    for copy in copies:
        copy.wait()


def call(body, out, *args, name, loads=(), scratch=(), flops=0, target=pltpu.VMEM):
    shapes = [jax.ShapeDtypeStruct(o, jnp.float32) if isinstance(o, tuple) else o for o in out]
    loads = [pltpu.with_memory_space_constraint(v, pltpu.HBM) for v in loads]
    return pl.pallas_call(
        body,
        out_shape=shapes,
        in_specs=[pl.BlockSpec(memory_space=pltpu.VMEM)] * len(args)
        + [pl.BlockSpec(memory_space=pltpu.HBM)] * len(loads),
        out_specs=[pl.BlockSpec(memory_space=target)] * len(shapes),
        scratch_shapes=scratch,
        compiler_params=pltpu.CompilerParams(vmem_limit_bytes=8 * 2**20),
        cost_estimate=pl.CostEstimate(flops=flops, bytes_accessed=2**20, transcendentals=0),
        name=name,
    )(*args, *loads)


def per_device(sizes, cot, ax, ay, az, cx, cy, cz, opened):
    x_rounds, y_rounds, z_rounds = (pair_rounds(sizes, d) for d in range(3))
    early_rounds = pair_rounds(sizes, 0, 1)
    x_rounds = pair_rounds(sizes, 0, 0)
    block = az.shape
    planes, rows, lanes = block
    swap = lambda value, perm: lax.ppermute(value, AXES, perm)
    packed = (rows // fold(planes, rows, lanes), lanes)
    dma = pltpu.SemaphoreType.DMA
    cot, opened, az, cz, w, edges, *z_out = call(
        functools.partial(z_pack, sizes, planes, rows, lanes),
        [block, jax.ShapeDtypeStruct(block, jnp.int32), block, block, block, (2, *packed)]
        + [packed] * len(z_rounds),
        loads=(cot, opened, az, cz),
        name="z_pack", scratch=[dma((4, planes))],
    )
    z_in = [swap(m, p) for m, p in zip(z_out, z_rounds)]
    (partial,) = call(z_inner, [block], cot, w, az, cz, name="z_inner")
    parts_y = call(y_factors, [block] * 5, ay, cy, name="y_factors")
    ends, *y_out = call(
        functools.partial(z_sweep, sizes),
        [packed] + [(planes, 8, lanes)] * len(y_rounds),
        partial, edges, opened, ay, cy, ax, cx, parts_y[0], *z_in,
        name="z_sweep",
    )
    y_in = [swap(m, p) for m, p in zip(y_out, y_rounds)]
    partial, w_rims, *x_out = call(
        functools.partial(y_inner, sizes),
        [block, (planes, 8, lanes)] + [(4 * rows + rows // 2, lanes)] * len(x_rounds),
        partial, ends, opened, ax, cx, *parts_y,
        name="y_inner",
    )
    x_early = [swap(m, p) for m, p in zip(x_out, early_rounds)]
    g, *x_out = call(
        functools.partial(y_sweep, sizes),
        [block] + [(16 + rows // 2, lanes)] * len(x_rounds),
        partial, w_rims, opened, ay, cy, cx, *y_in,
        name="y_sweep", flops=10**10,
    )
    x_late = [swap(m, p) for m, p in zip(x_out, x_rounds)]
    ready = call(
        x_inner, [(4, rows, lanes)] + [(planes - 2, rows, lanes)] * 2, g, opened, ax, cx, name="x_inner"
    )
    (out,) = call(
        functools.partial(x_sweep, sizes), [block], g, ax, cx, *ready, *x_early, *x_late,
        target=pltpu.HBM, name="x_sweep",
        scratch=[pltpu.VMEM(block, jnp.float32), dma((planes,))],
    )
    return out


def solution(mesh):
    sizes = tuple(mesh.shape[axis] for axis in AXES)
    placed = P(*AXES)
    return jax.shard_map(
        functools.partial(per_device, sizes),
        mesh=mesh,
        in_specs=(placed,) * 8,
        out_specs=placed,
        check_vma=False,
    )
```

```python
import functools
import itertools

import jax
import jax.numpy as jnp
from jax import lax
from jax.experimental import pallas as pl
from jax.experimental.pallas import tpu as pltpu
from jax.sharding import PartitionSpec as P

sharpness = 3.5
slot = 8
AXES = ("gx", "gy", "gz")


def colours(sizes, along):
    return min(sizes[along] - 1, 3 if along == 2 else 2)


def turn_of(face, along, n):
    return (face + (1 if along == 0 else 0)) % n


def pair_rounds(sizes, along, aside=0):
    n = colours(sizes, along)

    def partner(at, turn):
        at = list(at)
        i = at[along]
        if turn_of(i, along, n) == turn and i + 1 < sizes[along]:
            at[along] += 1
        elif i > 0 and turn_of(i - 1, along, n) == turn:
            at[along] -= 1
        elif aside == along:
            at[along] = sizes[along] - 1 - i
        elif sizes[aside] % 2 == 0:
            at[aside] ^= 1
        return at

    places = list(itertools.product(*(range(size) for size in sizes)))
    flat = lambda at: (at[0] * sizes[1] + at[1]) * sizes[2] + at[2]
    return [[(flat(at), flat(partner(at, turn))) for at in places] for turn in range(n)]


def to_send(sizes, along, up, down):
    n, at = colours(sizes, along), lax.axis_index(AXES[along])
    if n <= 1:
        return [jnp.where(at == 0, up, down)] * n
    mine = turn_of(at, along, n)
    return [jnp.where((mine == turn) & (at < sizes[along] - 1), up, down) for turn in range(n)]


def received(sizes, along, messages, like):
    n, at = colours(sizes, along), lax.axis_index(AXES[along])
    if n == 0:
        return jnp.zeros_like(like), jnp.zeros_like(like)
    low = high = messages[0]
    for turn in range(1, n):
        low = jnp.where(turn_of(at + n - 1, along, n) == turn, messages[turn], low)
        high = jnp.where(turn_of(at, along, n) == turn, messages[turn], high)
    return jnp.where(at > 0, low, 0.0), jnp.where(at < sizes[along] - 1, high, 0.0)


def bend(a, difference):
    t = jnp.tanh(sharpness * difference)
    return t, 0.5 * sharpness * a * (1.0 - a) * (1.0 - t * t)


def low_end(low, w0, w1, a0, a1, c0):
    w_far, w_low, a_far, a_low, c_far, c_low = low
    _, bent = bend(a_low, a0 - a_far)
    across = w0 - w_low
    r_low = (across * jnp.maximum(c_low, 0.0) - (w_low - w_far) * jnp.minimum(c_far, 0.0)) * bent
    forth = (w1 - w0) * jnp.maximum(c0, 0.0)
    back = across * jnp.minimum(c_low, 0.0)
    t, bent = bend(a0, a1 - a_low)
    first = w0 * (c0 - c_low) + (forth + back) + (forth - back) * ((0.5 - a0) * t) + r_low
    return first, (forth - back) * bent


def high_end(high, w0, w1, a0, a1, c0, c1):
    w_high, w_far, a_high, a_far, c_high = high
    _, bent = bend(a_high, a_far - a1)
    across = w_high - w1
    r_high = ((w_far - w_high) * jnp.maximum(c_high, 0.0) - across * jnp.minimum(c1, 0.0)) * bent
    forth = across * jnp.maximum(c1, 0.0)
    back = (w1 - w0) * jnp.minimum(c0, 0.0)
    t, bent = bend(a1, a_high - a0)
    last = w1 * (c1 - c0) + (forth + back) + (forth - back) * ((0.5 - a1) * t) - r_high
    return last, (back - forth) * bent


def factors(a, c, dim):
    length = a.shape[dim]
    at = lax.broadcasted_iota(jnp.int32, a.shape, dim)
    inside = (at > 0) & (at < length - 1)
    below = pltpu.roll(c, 1, dim)
    t, bent = bend(a, pltpu.roll(a, length - 1, dim) - pltpu.roll(a, 1, dim))
    return (
        jnp.where(inside, c - below, 0.0),
        jnp.where(inside, jnp.maximum(c, 0.0), 0.0),
        jnp.where(inside, jnp.minimum(below, 0.0), 0.0),
        (0.5 - a) * t,
        bent,
    )


def interior(g, w, parts, dim):
    rise, ahead, behind, lean, bent = parts
    length = w.shape[dim]
    prev = lambda value: pltpu.roll(value, 1, dim)
    after = lambda value: pltpu.roll(value, length - 1, dim)
    forth = (after(w) - w) * ahead
    back = (w - prev(w)) * behind
    apart = forth - back
    r = apart * bent
    return g + (w * rise + (forth + back) + apart * lean) + (prev(r) - after(r))


def fold(planes, rows, lanes):
    per = lanes // (slot * planes)
    return per if per >= 1 and rows % (8 * per) == 0 else 1


def edge_lanes(shape, lanes):
    at = lax.broadcasted_iota(jnp.int32, shape, 1)
    return at, lax.rem(at, slot)


def z_pack(sizes, planes, rows, lanes, *refs):
    sources, targets, (w_ref, edge_ref, *out, sems) = refs[:4], refs[4:8], refs[8:]
    copies = [
        [
            pltpu.make_async_copy(src.at[x], dst.at[x], sems.at[n, x])
            for n, (src, dst) in enumerate(zip(sources, targets))
        ]
        for x in range(planes)
    ]
    for copy in itertools.chain(*copies):
        copy.start()
    cot, opened, a_ref, c_ref = targets
    per = fold(planes, rows, lanes)
    step = rows // per
    at, place = edge_lanes((rows, lanes), lanes)
    near = (at < 2) | (at >= lanes - 2)
    totals = [None] * 2
    for x in range(planes):
        for copy in itertools.chain(*({0: copies[:2], 2: copies[2:]}.get(x, []))):
            copy.wait()
        w = cot[x] * opened[x].astype(jnp.float32)
        w_ref[x] = w
        for n, field, lane in ((0, w, 2), (0, a_ref[x], 6), (1, c_ref[x], 4)):
            field = jnp.where(near, field, 0.0)
            for r in range(per):
                part = field[r * step : (r + 1) * step]
                part = pltpu.roll(part, (slot * (x + planes * r) + lane) % lanes, 1)
                totals[n] = part if totals[n] is None else totals[n] + part
    for n in range(2):
        edge_ref[n] = totals[n]
    _, place = edge_lanes((step, lanes), lanes)
    up = jnp.where(lax.rem(place, 4) < 2, totals[0], jnp.where(place < 4, totals[1], 0.0))
    down = jnp.where(lax.rem(place, 4) >= 2, totals[0], jnp.where(place >= 4, totals[1], 0.0))
    for ref, message in zip(out, to_send(sizes, 2, up, down)):
        ref[...] = message


def z_inner(g_ref, w_ref, a_ref, c_ref, out):
    for x in range(a_ref.shape[0]):
        out[x] = interior(g_ref[x], w_ref[x], factors(a_ref[x], c_ref[x], 1), 1)


def y_factors(ay, cy, *out):
    for x in range(ay.shape[0]):
        for ref, part in zip(out, factors(ay[x], cy[x], 0)):
            ref[x] = part


def z_ends(edges, low, high, lanes):
    lane = lambda value, at: pltpu.roll(value, lanes - at, 1) if at else value
    wa, c = edges
    w_far, w_low, c_far, c_low, a_far, a_low = (lane(low, at) for at in range(6))
    first, second = low_end(
        (w_far, w_low, a_far, a_low, c_far, c_low),
        *(lane(wa, at) for at in (2, 3, 6, 7)),
        lane(c, 4),
    )
    w_high, w_far, c_high, a_high, a_far = (lane(high, at) for at in (2, 3, 4, 6, 7))
    last, before = high_end(
        (w_high, w_far, a_high, a_far, c_high),
        *(lane(wa, at) for at in (0, 1, 4, 5)),
        *(lane(c, at) for at in (2, 3)),
    )
    return first, second, last, before


columns = (0, 1, -1, -2)


def spread(ends, x, r, planes, lanes, column=0):
    move = (column - slot * (x + planes * r)) % lanes
    return pltpu.roll(ends, move, 1) if move else ends


def on_columns(at, lanes, values):
    total = 0.0
    for column, value in zip(columns, values):
        total = jnp.where(at == column % lanes, value, total)
    return total


def z_sweep(sizes, partial, edges, opened, ay, cy, ax, cx, _, *rest):
    n_in = colours(sizes, 2)
    messages, (ends_ref, *out) = [m[...] for m in rest[:n_in]], rest[n_in:]
    planes, rows, lanes = ay.shape
    per = fold(planes, rows, lanes)
    step = rows // per
    low, high = received(sizes, 2, messages, edges[0])
    ends = z_ends([edges[0], edges[1]], low, high, lanes)
    _, place = edge_lanes((step, lanes), lanes)
    ends_ref[...] = on_columns(
        place, slot, [spread(end, 0, 0, planes, lanes, column) for end, column in zip(ends, columns)]
    )
    if not out:
        return
    at = lax.broadcasted_iota(jnp.int32, (8, lanes), 1)
    tile = lax.broadcasted_iota(jnp.int32, (8, lanes), 0)
    for x in range(planes):
        ws = []
        for rim, group, r in ((slice(0, 8), slice(0, 8), 0), (slice(rows - 8, rows), slice(step - 8, step), per - 1)):
            added = [
                spread(end[group], x, r, planes, lanes, column) for end, column in zip(ends, columns)
            ]
            g = partial[x, rim] + on_columns(at, lanes, added)
            ws.append(opened[x, rim].astype(jnp.float32) * g)
        a, c = (pltpu.roll(ref[x, rows - 8 :], by, 0) for ref, by in ((ay, 6), (cy, 4)))
        up = jnp.where(tile >= 6, ws[1], jnp.where(tile >= 4, a, c))
        a, c = (pltpu.roll(ref[x, :8], by, 0) for ref, by in ((ay, 2), (cy, 4)))
        down = jnp.where(tile < 2, ws[0], jnp.where(tile < 4, a, c))
        for ref, message in zip(out, to_send(sizes, 1, up, down)):
            ref[x] = message


def x_products(w, cx):
    planes = len(w)
    back = (w[-1] - w[-2]) * jnp.minimum(cx[planes - 2], 0.0)
    forth = (w[1] - w[0]) * jnp.maximum(cx[0], 0.0)
    return (w[-1], w[0]), (back, forth)


def early_rows(rows):
    return rows * 5 // 64 * 8


def y_inner(sizes, partial_z, ends_ref, opened, ax, cx, *rest):
    parts_y, (partial, w_rims, *out) = rest[:5], rest[5:]
    planes, rows, lanes = ax.shape
    ends = ends_ref[...]
    at = lax.broadcasted_iota(jnp.int32, (rows, lanes), 1)
    near = (at < 2) | (at >= lanes - 2)
    tile = lax.broadcasted_iota(jnp.int32, (8, lanes), 0)
    per = fold(planes, rows, lanes)
    ws = []
    for x in range(planes):
        mask = opened[x].astype(jnp.float32)
        parts = jnp.concatenate([spread(ends, x, r, planes, lanes) for r in range(per)], axis=0)
        g = partial_z[x] + jnp.where(near, parts, 0.0)
        w = mask * g
        w_rims[x] = jnp.where(tile < 4, w[:8], w[rows - 8 :])
        g = interior(g, w, [part[x] for part in parts_y], 0)
        partial[x] = g
        ws.append(mask * g)
    pairs = (
        *x_products(ws, cx),
        (ax[planes - 2], ax[0]),
        (ax[planes - 1], ax[1]),
    )
    for v, (up, down) in enumerate(pairs):
        for ref, message in zip(out, to_send(sizes, 0, up, down)):
            ref[v * rows : (v + 1) * rows] = message
    half = slice(0, early_rows(rows))
    for ref, message in zip(out, to_send(sizes, 0, cx[planes - 1, half], cx[0, half])):
        ref[4 * rows :] = message


def y_sweep(sizes, partial, w_rims, opened, ay, cy, cx, *rest):
    n_in = colours(sizes, 1)
    messages, (g_ref, *out) = rest[:n_in], rest[n_in:]
    planes, rows, lanes = ay.shape
    tile = lax.broadcasted_iota(jnp.int32, (8, lanes), 0)
    ws = []
    for x in range(planes):
        low, high = received(sizes, 1, [m[x] for m in messages], ay[x, :8])
        row = lambda ref, n: ref[x, n : n + 1]
        first, second = low_end(
            [low[v : v + 1] for v in (6, 7, 4, 5, 2, 3)],
            *(row(ref, n) for ref, n in ((w_rims, 0), (w_rims, 1), (ay, 0), (ay, 1), (cy, 0))),
        )
        last, before = high_end(
            [high[v : v + 1] for v in range(5)],
            row(w_rims, 6),
            row(w_rims, 7),
            *(row(ref, n) for ref in (ay, cy) for n in (rows - 2, rows - 1)),
        )
        top = partial[x, :8] + jnp.where(tile == 0, first, jnp.where(tile == 1, second, 0.0))
        bottom = partial[x, rows - 8 :] + jnp.where(
            tile == 7, last, jnp.where(tile == 6, before, 0.0)
        )
        g_ref[x, :8] = top
        g_ref[x, 8 : rows - 8] = partial[x, 8 : rows - 8]
        g_ref[x, rows - 8 :] = bottom
        mask = jnp.where(tile < 4, opened[x, :8], opened[x, rows - 8 :]).astype(jnp.float32)
        ws.append(mask * jnp.where(tile < 4, top, bottom))
    if out:
        c = [jnp.where(tile < 4, cx[x, :8], cx[x, rows - 8 :]) for x in range(planes)]
        for v, (up, down) in enumerate(x_products(ws, c)):
            for ref, message in zip(out, to_send(sizes, 0, up, down)):
                ref[8 * v : 8 * v + 8] = message
        half = slice(early_rows(rows), rows)
        for ref, message in zip(out, to_send(sizes, 0, cx[planes - 1, half], cx[0, half])):
            ref[16:] = message


def x_inner(g_ref, opened, ax, cx, ready, own_ref, r_ref):
    planes = ax.shape[0]
    last = planes - 1
    w = [opened[x].astype(jnp.float32) * g_ref[x] for x in range(planes)]
    ready[0], ready[1] = w[0], w[last]
    ready[2] = (w[1] - w[0]) * jnp.maximum(cx[0], 0.0)
    ready[3] = (w[last] - w[last - 1]) * jnp.minimum(cx[last - 1], 0.0)
    for x in range(1, last):
        t, bent = bend(ax[x], ax[x + 1] - ax[x - 1])
        forth = (w[x + 1] - w[x]) * jnp.maximum(cx[x], 0.0)
        back = (w[x] - w[x - 1]) * jnp.minimum(cx[x - 1], 0.0)
        apart = forth - back
        r_ref[x - 1] = apart * bent
        own_ref[x - 1] = (
            g_ref[x] + w[x] * (cx[x] - cx[x - 1]) + (forth + back) + apart * ((0.5 - ax[x]) * t)
        )


def x_sweep(sizes, g_ref, ax, cx, ready, own_ref, r_ref, *rest):
    n_in = colours(sizes, 0)
    early, late, (out, stage, sems) = rest[:n_in], rest[n_in : 2 * n_in], rest[2 * n_in :]
    planes, rows, lanes = ax.shape
    last = planes - 1
    tile = lax.broadcasted_iota(jnp.int32, (8, lanes), 0)

    def whole(n, v):
        if v == 4:
            return jnp.concatenate([early[n][4 * rows :], late[n][16:]], axis=0)
        value = early[n][v * rows : (v + 1) * rows]
        if v > 1:
            return value
        ends = late[n][8 * v : 8 * v + 8]
        top = jnp.where(tile < 2, ends, value[:8])
        bottom = jnp.where(tile >= 6, ends, value[rows - 8 :])
        return jnp.concatenate([top, value[8 : rows - 8], bottom], axis=0)

    (w_low, w_high), (b_low, f_high), (f0, h0), (f1, h1), (c_low, _) = (
        received(sizes, 0, [whole(n, v) for n in range(n_in)], ax[0]) for v in range(5)
    )
    copies = []

    def leave(x, value):
        stage[x] = value
        copies.append(pltpu.make_async_copy(stage.at[x], out.at[x], sems.at[x]))
        copies[-1].start()

    def outer(x, w, a_next, forth, back, c_low):
        t, bent = bend(ax[x], a_next)
        apart = forth - back
        own = g_ref[x] + w * (cx[x] - c_low) + (forth + back) + apart * ((0.5 - ax[x]) * t)
        return own, apart * bent

    w_first, w_last = ready[0], ready[1]
    across = w_first - w_low
    own_first, r_first = outer(
        0, w_first, ax[1] - f1, ready[2], across * jnp.minimum(c_low, 0.0), c_low
    )
    _, bent = bend(f1, ax[0] - f0)
    r_low = (across * jnp.maximum(c_low, 0.0) - b_low) * bent
    across = w_high - w_last
    own_last, r_last = outer(
        last, w_last, h0 - ax[last - 1], across * jnp.maximum(cx[last], 0.0), ready[3], cx[last - 1]
    )
    _, bent = bend(h0, h1 - ax[last])
    r_high = (f_high - across * jnp.minimum(cx[last], 0.0)) * bent
    r = [r_low, r_first, *(r_ref[x] for x in range(last - 1)), r_last, r_high]
    for x in range(planes):
        own = own_first if x == 0 else own_last if x == last else own_ref[x - 1]
        leave(x, own + (r[x] - r[x + 2]))
    for copy in copies:
        copy.wait()


def call(body, out, *args, name, loads=(), scratch=(), flops=0, target=pltpu.VMEM):
    shapes = [jax.ShapeDtypeStruct(o, jnp.float32) if isinstance(o, tuple) else o for o in out]
    loads = [pltpu.with_memory_space_constraint(v, pltpu.HBM) for v in loads]
    return pl.pallas_call(
        body,
        out_shape=shapes,
        in_specs=[pl.BlockSpec(memory_space=pltpu.VMEM)] * len(args)
        + [pl.BlockSpec(memory_space=pltpu.HBM)] * len(loads),
        out_specs=[pl.BlockSpec(memory_space=target)] * len(shapes),
        scratch_shapes=scratch,
        compiler_params=pltpu.CompilerParams(vmem_limit_bytes=8 * 2**20),
        cost_estimate=pl.CostEstimate(flops=flops, bytes_accessed=2**20, transcendentals=0),
        name=name,
    )(*args, *loads)


def per_device(sizes, cot, ax, ay, az, cx, cy, cz, opened):
    x_rounds, y_rounds, z_rounds = (pair_rounds(sizes, d) for d in range(3))
    early_rounds = pair_rounds(sizes, 0, 1)
    x_rounds = pair_rounds(sizes, 0, 0)
    block = az.shape
    planes, rows, lanes = block
    swap = lambda value, perm: lax.ppermute(value, AXES, perm)
    packed = (rows // fold(planes, rows, lanes), lanes)
    dma = pltpu.SemaphoreType.DMA
    cot, opened, az, cz, w, edges, *z_out = call(
        functools.partial(z_pack, sizes, planes, rows, lanes),
        [block, jax.ShapeDtypeStruct(block, jnp.int32), block, block, block, (2, *packed)]
        + [packed] * len(z_rounds),
        loads=(cot, opened, az, cz),
        name="z_pack", scratch=[dma((4, planes))],
    )
    z_in = [swap(m, p) for m, p in zip(z_out, z_rounds)]
    (partial,) = call(z_inner, [block], cot, w, az, cz, name="z_inner")
    parts_y = call(y_factors, [block] * 5, ay, cy, name="y_factors")
    ends, *y_out = call(
        functools.partial(z_sweep, sizes),
        [packed] + [(planes, 8, lanes)] * len(y_rounds),
        partial, edges, opened, ay, cy, ax, cx, parts_y[0], *z_in,
        name="z_sweep",
    )
    y_in = [swap(m, p) for m, p in zip(y_out, y_rounds)]
    partial, w_rims, *x_out = call(
        functools.partial(y_inner, sizes),
        [block, (planes, 8, lanes)] + [(4 * rows + early_rows(rows), lanes)] * len(x_rounds),
        partial, ends, opened, ax, cx, *parts_y,
        name="y_inner",
    )
    x_early = [swap(m, p) for m, p in zip(x_out, early_rounds)]
    g, *x_out = call(
        functools.partial(y_sweep, sizes),
        [block] + [(16 + rows - early_rows(rows), lanes)] * len(x_rounds),
        partial, w_rims, opened, ay, cy, cx, *y_in,
        name="y_sweep", flops=10**10,
    )
    x_late = [swap(m, p) for m, p in zip(x_out, x_rounds)]
    ready = call(
        x_inner, [(4, rows, lanes)] + [(planes - 2, rows, lanes)] * 2, g, opened, ax, cx, name="x_inner"
    )
    (out,) = call(
        functools.partial(x_sweep, sizes), [block], g, ax, cx, *ready, *x_early, *x_late,
        target=pltpu.HBM, name="x_sweep",
        scratch=[pltpu.VMEM(block, jnp.float32), dma((planes,))],
    )
    return out


def solution(mesh):
    sizes = tuple(mesh.shape[axis] for axis in AXES)
    placed = P(*AXES)
    return jax.shard_map(
        functools.partial(per_device, sizes),
        mesh=mesh,
        in_specs=(placed,) * 8,
        out_specs=placed,
        check_vma=False,
    )
```

```python
import functools
import itertools

import jax
import jax.numpy as jnp
from jax import lax
from jax.experimental import pallas as pl
from jax.experimental.pallas import tpu as pltpu
from jax.sharding import PartitionSpec as P

sharpness = 3.5
slot = 8
AXES = ("gx", "gy", "gz")


def colours(sizes, along):
    return min(sizes[along] - 1, 3 if along == 2 else 2)


def turn_of(face, along, n):
    return (face + (1 if along == 0 else 0)) % n


def pair_rounds(sizes, along, aside=0):
    n = colours(sizes, along)

    def partner(at, turn):
        at = list(at)
        i = at[along]
        if turn_of(i, along, n) == turn and i + 1 < sizes[along]:
            at[along] += 1
        elif i > 0 and turn_of(i - 1, along, n) == turn:
            at[along] -= 1
        elif aside == along:
            at[along] = sizes[along] - 1 - i
        elif sizes[aside] % 2 == 0:
            at[aside] ^= 1
        return at

    places = list(itertools.product(*(range(size) for size in sizes)))
    flat = lambda at: (at[0] * sizes[1] + at[1]) * sizes[2] + at[2]
    return [[(flat(at), flat(partner(at, turn))) for at in places] for turn in range(n)]


def to_send(sizes, along, up, down):
    n, at = colours(sizes, along), lax.axis_index(AXES[along])
    if n <= 1:
        return [jnp.where(at == 0, up, down)] * n
    mine = turn_of(at, along, n)
    return [jnp.where((mine == turn) & (at < sizes[along] - 1), up, down) for turn in range(n)]


def received(sizes, along, messages, like):
    n, at = colours(sizes, along), lax.axis_index(AXES[along])
    if n == 0:
        return jnp.zeros_like(like), jnp.zeros_like(like)
    low = high = messages[0]
    for turn in range(1, n):
        low = jnp.where(turn_of(at + n - 1, along, n) == turn, messages[turn], low)
        high = jnp.where(turn_of(at, along, n) == turn, messages[turn], high)
    return jnp.where(at > 0, low, 0.0), jnp.where(at < sizes[along] - 1, high, 0.0)


def bend(a, difference):
    t = jnp.tanh(sharpness * difference)
    return t, 0.5 * sharpness * a * (1.0 - a) * (1.0 - t * t)


def low_end(low, w0, w1, a0, a1, c0):
    w_far, w_low, a_far, a_low, c_far, c_low = low
    _, bent = bend(a_low, a0 - a_far)
    across = w0 - w_low
    r_low = (across * jnp.maximum(c_low, 0.0) - (w_low - w_far) * jnp.minimum(c_far, 0.0)) * bent
    forth = (w1 - w0) * jnp.maximum(c0, 0.0)
    back = across * jnp.minimum(c_low, 0.0)
    t, bent = bend(a0, a1 - a_low)
    first = w0 * (c0 - c_low) + (forth + back) + (forth - back) * ((0.5 - a0) * t) + r_low
    return first, (forth - back) * bent


def high_end(high, w0, w1, a0, a1, c0, c1):
    w_high, w_far, a_high, a_far, c_high = high
    _, bent = bend(a_high, a_far - a1)
    across = w_high - w1
    r_high = ((w_far - w_high) * jnp.maximum(c_high, 0.0) - across * jnp.minimum(c1, 0.0)) * bent
    forth = across * jnp.maximum(c1, 0.0)
    back = (w1 - w0) * jnp.minimum(c0, 0.0)
    t, bent = bend(a1, a_high - a0)
    last = w1 * (c1 - c0) + (forth + back) + (forth - back) * ((0.5 - a1) * t) - r_high
    return last, (back - forth) * bent


def factors(a, c, dim):
    length = a.shape[dim]
    at = lax.broadcasted_iota(jnp.int32, a.shape, dim)
    inside = (at > 0) & (at < length - 1)
    below = pltpu.roll(c, 1, dim)
    t, bent = bend(a, pltpu.roll(a, length - 1, dim) - pltpu.roll(a, 1, dim))
    return (
        jnp.where(inside, c - below, 0.0),
        jnp.where(inside, jnp.maximum(c, 0.0), 0.0),
        jnp.where(inside, jnp.minimum(below, 0.0), 0.0),
        (0.5 - a) * t,
        bent,
    )


def interior(g, w, parts, dim):
    rise, ahead, behind, lean, bent = parts
    length = w.shape[dim]
    prev = lambda value: pltpu.roll(value, 1, dim)
    after = lambda value: pltpu.roll(value, length - 1, dim)
    forth = (after(w) - w) * ahead
    back = (w - prev(w)) * behind
    apart = forth - back
    r = apart * bent
    return g + (w * rise + (forth + back) + apart * lean) + (prev(r) - after(r))


def fold(planes, rows, lanes):
    per = lanes // (slot * planes)
    return per if per >= 1 and rows % (8 * per) == 0 else 1


def edge_lanes(shape, lanes):
    at = lax.broadcasted_iota(jnp.int32, shape, 1)
    return at, lax.rem(at, slot)


def z_pack(sizes, planes, rows, lanes, *refs):
    sources, targets, (w_ref, edge_ref, *out, sems) = refs[:4], refs[4:8], refs[8:]
    copies = [
        [
            pltpu.make_async_copy(src.at[x], dst.at[x], sems.at[n, x])
            for n, (src, dst) in enumerate(zip(sources, targets))
        ]
        for x in range(planes)
    ]
    for copy in itertools.chain(*copies):
        copy.start()
    cot, opened, a_ref, c_ref = targets
    per = fold(planes, rows, lanes)
    step = rows // per
    at, place = edge_lanes((rows, lanes), lanes)
    near = (at < 2) | (at >= lanes - 2)
    totals = [None] * 2
    for x in range(planes):
        for copy in itertools.chain(*({0: copies[:2], 2: copies[2:]}.get(x, []))):
            copy.wait()
        w = cot[x] * opened[x].astype(jnp.float32)
        w_ref[x] = w
        for n, field, lane in ((0, w, 2), (0, a_ref[x], 6), (1, c_ref[x], 4)):
            field = jnp.where(near, field, 0.0)
            for r in range(per):
                part = field[r * step : (r + 1) * step]
                part = pltpu.roll(part, (slot * (x + planes * r) + lane) % lanes, 1)
                totals[n] = part if totals[n] is None else totals[n] + part
    for n in range(2):
        edge_ref[n] = totals[n]
    _, place = edge_lanes((step, lanes), lanes)
    up = jnp.where(lax.rem(place, 4) < 2, totals[0], jnp.where(place < 4, totals[1], 0.0))
    down = jnp.where(lax.rem(place, 4) >= 2, totals[0], jnp.where(place >= 4, totals[1], 0.0))
    for ref, message in zip(out, to_send(sizes, 2, up, down)):
        ref[...] = message


def lane(value, at):
    lanes = value.shape[1]
    return pltpu.roll(value, lanes - at, 1) if at else value


def z_inner(g_ref, w_ref, a_ref, c_ref, edges, out, own):
    for x in range(a_ref.shape[0]):
        out[x] = interior(g_ref[x], w_ref[x], factors(a_ref[x], c_ref[x], 1), 1)
    for n, at in enumerate((2, 3, 6, 7, 0, 1, 4, 5)):
        own[n] = lane(edges[0], at)
    for n, at in enumerate((4, 2, 3)):
        own[8 + n] = lane(edges[1], at)


def y_factors(sizes, ay, cy, *out):
    planes, rows, lanes = ay.shape
    tile = lax.broadcasted_iota(jnp.int32, (8, lanes), 0)
    for x in range(planes):
        for ref, part in zip(out, factors(ay[x], cy[x], 0)):
            ref[x] = part
        a, c = (pltpu.roll(ref[x, rows - 8 :], by, 0) for ref, by in ((ay, 6), (cy, 4)))
        up = jnp.where(tile >= 4, a, c)
        a, c = (pltpu.roll(ref[x, :8], by, 0) for ref, by in ((ay, 2), (cy, 4)))
        down = jnp.where(tile < 4, a, c)
        for ref, message in zip(out[5:], to_send(sizes, 1, up, down)):
            ref[x] = message


def z_ends(own, low, high):
    w_far, w_low, c_far, c_low, a_far, a_low = (lane(low, at) for at in range(6))
    first, second = low_end((w_far, w_low, a_far, a_low, c_far, c_low), *own[:4], own[8])
    w_high, w_far, c_high, a_high, a_far = (lane(high, at) for at in (2, 3, 4, 6, 7))
    last, before = high_end((w_high, w_far, a_high, a_far, c_high), *own[4:8], *own[9:])
    return first, second, last, before


columns = (0, 1, -1, -2)


def spread(ends, x, r, planes, lanes, column=0):
    move = (column - slot * (x + planes * r)) % lanes
    return pltpu.roll(ends, move, 1) if move else ends


def on_columns(at, lanes, values):
    total = 0.0
    for column, value in zip(columns, values):
        total = jnp.where(at == column % lanes, value, total)
    return total


def z_sweep(sizes, partial, own, opened, ax, cx, *rest):
    n_in, n_y = colours(sizes, 2), colours(sizes, 1)
    others, messages = rest[:n_y], [m[...] for m in rest[n_y : n_y + n_in]]
    ends_ref, *out = rest[n_y + n_in :]
    planes, rows, lanes = partial.shape
    per = fold(planes, rows, lanes)
    step = rows // per
    low, high = received(sizes, 2, messages, own[0])
    ends = z_ends([own[n] for n in range(11)], low, high)
    _, place = edge_lanes((step, lanes), lanes)
    ends_ref[...] = on_columns(
        place, slot, [spread(end, 0, 0, planes, lanes, column) for end, column in zip(ends, columns)]
    )
    if not out:
        return
    at = lax.broadcasted_iota(jnp.int32, (8, lanes), 1)
    tile = lax.broadcasted_iota(jnp.int32, (8, lanes), 0)
    for x in range(planes):
        ws = []
        for rim, group, r in ((slice(0, 8), slice(0, 8), 0), (slice(rows - 8, rows), slice(step - 8, step), per - 1)):
            added = [
                spread(end[group], x, r, planes, lanes, column) for end, column in zip(ends, columns)
            ]
            g = partial[x, rim] + on_columns(at, lanes, added)
            ws.append(opened[x, rim].astype(jnp.float32) * g)
        row = to_send(sizes, 1, tile, 7 - tile)
        for other, ref, here, w in zip(others, out, row, to_send(sizes, 1, ws[1], ws[0])):
            ref[x] = jnp.where(here >= 6, w, other[x])


def x_products(w, cx):
    planes = len(w)
    back = (w[-1] - w[-2]) * jnp.minimum(cx[planes - 2], 0.0)
    forth = (w[1] - w[0]) * jnp.maximum(cx[0], 0.0)
    return (w[-1], w[0]), (back, forth)


def early_rows(rows):
    return rows * 5 // 64 * 8


def y_inner(sizes, partial_z, ends_ref, opened, ax, cx, *rest):
    parts_y, (partial, w_rims, *out) = rest[:5], rest[5:]
    planes, rows, lanes = ax.shape
    ends = ends_ref[...]
    at = lax.broadcasted_iota(jnp.int32, (rows, lanes), 1)
    near = (at < 2) | (at >= lanes - 2)
    tile = lax.broadcasted_iota(jnp.int32, (8, lanes), 0)
    per = fold(planes, rows, lanes)
    ws = []
    for x in range(planes):
        mask = opened[x].astype(jnp.float32)
        parts = jnp.concatenate([spread(ends, x, r, planes, lanes) for r in range(per)], axis=0)
        g = partial_z[x] + jnp.where(near, parts, 0.0)
        w = mask * g
        w_rims[x] = jnp.where(tile < 4, w[:8], w[rows - 8 :])
        g = interior(g, w, [part[x] for part in parts_y], 0)
        partial[x] = g
        ws.append(mask * g)
    pairs = (
        *x_products(ws, cx),
        (ax[planes - 2], ax[0]),
        (ax[planes - 1], ax[1]),
    )
    for v, (up, down) in enumerate(pairs):
        for ref, message in zip(out, to_send(sizes, 0, up, down)):
            ref[v * rows : (v + 1) * rows] = message
    half = slice(0, early_rows(rows))
    for ref, message in zip(out, to_send(sizes, 0, cx[planes - 1, half], cx[0, half])):
        ref[4 * rows :] = message


def y_sweep(sizes, partial, w_rims, opened, ay, cy, cx, *rest):
    n_in = colours(sizes, 1)
    messages, (g_ref, *out) = rest[:n_in], rest[n_in:]
    planes, rows, lanes = ay.shape
    tile = lax.broadcasted_iota(jnp.int32, (8, lanes), 0)
    ws = []
    for x in range(planes):
        low, high = received(sizes, 1, [m[x] for m in messages], ay[x, :8])
        row = lambda ref, n: ref[x, n : n + 1]
        first, second = low_end(
            [low[v : v + 1] for v in (6, 7, 4, 5, 2, 3)],
            *(row(ref, n) for ref, n in ((w_rims, 0), (w_rims, 1), (ay, 0), (ay, 1), (cy, 0))),
        )
        last, before = high_end(
            [high[v : v + 1] for v in range(5)],
            row(w_rims, 6),
            row(w_rims, 7),
            *(row(ref, n) for ref in (ay, cy) for n in (rows - 2, rows - 1)),
        )
        top = partial[x, :8] + jnp.where(tile == 0, first, jnp.where(tile == 1, second, 0.0))
        bottom = partial[x, rows - 8 :] + jnp.where(
            tile == 7, last, jnp.where(tile == 6, before, 0.0)
        )
        g_ref[x, :8] = top
        g_ref[x, 8 : rows - 8] = partial[x, 8 : rows - 8]
        g_ref[x, rows - 8 :] = bottom
        mask = jnp.where(tile < 4, opened[x, :8], opened[x, rows - 8 :]).astype(jnp.float32)
        ws.append(mask * jnp.where(tile < 4, top, bottom))
    if out:
        c = [jnp.where(tile < 4, cx[x, :8], cx[x, rows - 8 :]) for x in range(planes)]
        for v, (up, down) in enumerate(x_products(ws, c)):
            for ref, message in zip(out, to_send(sizes, 0, up, down)):
                ref[8 * v : 8 * v + 8] = message
        half = slice(early_rows(rows), rows)
        for ref, message in zip(out, to_send(sizes, 0, cx[planes - 1, half], cx[0, half])):
            ref[16:] = message


def x_inner(g_ref, opened, ax, cx, ready, own_ref, r_ref):
    planes = ax.shape[0]
    last = planes - 1
    w = [opened[x].astype(jnp.float32) * g_ref[x] for x in range(planes)]
    ready[0], ready[1] = w[0], w[last]
    ready[2] = (w[1] - w[0]) * jnp.maximum(cx[0], 0.0)
    ready[3] = (w[last] - w[last - 1]) * jnp.minimum(cx[last - 1], 0.0)
    for x in range(1, last):
        t, bent = bend(ax[x], ax[x + 1] - ax[x - 1])
        forth = (w[x + 1] - w[x]) * jnp.maximum(cx[x], 0.0)
        back = (w[x] - w[x - 1]) * jnp.minimum(cx[x - 1], 0.0)
        apart = forth - back
        r_ref[x - 1] = apart * bent
        own_ref[x - 1] = (
            g_ref[x] + w[x] * (cx[x] - cx[x - 1]) + (forth + back) + apart * ((0.5 - ax[x]) * t)
        )


def x_sweep(sizes, g_ref, ax, cx, ready, own_ref, r_ref, *rest):
    n_in = colours(sizes, 0)
    early, late, (out, stage, sems) = rest[:n_in], rest[n_in : 2 * n_in], rest[2 * n_in :]
    planes, rows, lanes = ax.shape
    last = planes - 1
    tile = lax.broadcasted_iota(jnp.int32, (8, lanes), 0)

    def whole(n, v):
        if v == 4:
            return jnp.concatenate([early[n][4 * rows :], late[n][16:]], axis=0)
        value = early[n][v * rows : (v + 1) * rows]
        if v > 1:
            return value
        ends = late[n][8 * v : 8 * v + 8]
        top = jnp.where(tile < 2, ends, value[:8])
        bottom = jnp.where(tile >= 6, ends, value[rows - 8 :])
        return jnp.concatenate([top, value[8 : rows - 8], bottom], axis=0)

    (w_low, w_high), (b_low, f_high), (f0, h0), (f1, h1), (c_low, _) = (
        received(sizes, 0, [whole(n, v) for n in range(n_in)], ax[0]) for v in range(5)
    )
    copies = []

    def leave(x, value):
        stage[x] = value
        copies.append(pltpu.make_async_copy(stage.at[x], out.at[x], sems.at[x]))
        copies[-1].start()

    def outer(x, w, a_next, forth, back, c_low):
        t, bent = bend(ax[x], a_next)
        apart = forth - back
        own = g_ref[x] + w * (cx[x] - c_low) + (forth + back) + apart * ((0.5 - ax[x]) * t)
        return own, apart * bent

    w_first, w_last = ready[0], ready[1]
    across = w_first - w_low
    own_first, r_first = outer(
        0, w_first, ax[1] - f1, ready[2], across * jnp.minimum(c_low, 0.0), c_low
    )
    _, bent = bend(f1, ax[0] - f0)
    r_low = (across * jnp.maximum(c_low, 0.0) - b_low) * bent
    across = w_high - w_last
    own_last, r_last = outer(
        last, w_last, h0 - ax[last - 1], across * jnp.maximum(cx[last], 0.0), ready[3], cx[last - 1]
    )
    _, bent = bend(h0, h1 - ax[last])
    r_high = (f_high - across * jnp.minimum(cx[last], 0.0)) * bent
    r = [r_low, r_first, *(r_ref[x] for x in range(last - 1)), r_last, r_high]
    for x in range(planes):
        own = own_first if x == 0 else own_last if x == last else own_ref[x - 1]
        leave(x, own + (r[x] - r[x + 2]))
    for copy in copies:
        copy.wait()


def call(body, out, *args, name, loads=(), scratch=(), flops=0, target=pltpu.VMEM):
    shapes = [jax.ShapeDtypeStruct(o, jnp.float32) if isinstance(o, tuple) else o for o in out]
    loads = [pltpu.with_memory_space_constraint(v, pltpu.HBM) for v in loads]
    return pl.pallas_call(
        body,
        out_shape=shapes,
        in_specs=[pl.BlockSpec(memory_space=pltpu.VMEM)] * len(args)
        + [pl.BlockSpec(memory_space=pltpu.HBM)] * len(loads),
        out_specs=[pl.BlockSpec(memory_space=target)] * len(shapes),
        scratch_shapes=scratch,
        compiler_params=pltpu.CompilerParams(vmem_limit_bytes=8 * 2**20),
        cost_estimate=pl.CostEstimate(flops=flops, bytes_accessed=2**20, transcendentals=0),
        name=name,
    )(*args, *loads)


def per_device(sizes, cot, ax, ay, az, cx, cy, cz, opened):
    x_rounds, y_rounds, z_rounds = (pair_rounds(sizes, d) for d in range(3))
    early_rounds = pair_rounds(sizes, 0, 1)
    x_rounds = pair_rounds(sizes, 0, 0)
    block = az.shape
    planes, rows, lanes = block
    swap = lambda value, perm: lax.ppermute(value, AXES, perm)
    packed = (rows // fold(planes, rows, lanes), lanes)
    dma = pltpu.SemaphoreType.DMA
    cot, opened, az, cz, w, edges, *z_out = call(
        functools.partial(z_pack, sizes, planes, rows, lanes),
        [block, jax.ShapeDtypeStruct(block, jnp.int32), block, block, block, (2, *packed)]
        + [packed] * len(z_rounds),
        loads=(cot, opened, az, cz),
        name="z_pack", scratch=[dma((4, planes))],
    )
    z_in = [swap(m, p) for m, p in zip(z_out, z_rounds)]
    partial, own = call(z_inner, [block, (11, *packed)], cot, w, az, cz, edges, name="z_inner")
    factors_y = call(
        functools.partial(y_factors, sizes),
        [block] * 5 + [(planes, 8, lanes)] * len(y_rounds),
        ay, cy,
        name="y_factors",
    )
    parts_y, others_y = factors_y[:5], factors_y[5:]
    ends, *y_out = call(
        functools.partial(z_sweep, sizes),
        [packed] + [(planes, 8, lanes)] * len(y_rounds),
        partial, own, opened, ax, cx, *others_y, *z_in,
        name="z_sweep",
    )
    y_in = [swap(m, p) for m, p in zip(y_out, y_rounds)]
    partial, w_rims, *x_out = call(
        functools.partial(y_inner, sizes),
        [block, (planes, 8, lanes)] + [(4 * rows + early_rows(rows), lanes)] * len(x_rounds),
        partial, ends, opened, ax, cx, *parts_y,
        name="y_inner",
    )
    x_early = [swap(m, p) for m, p in zip(x_out, early_rounds)]
    g, *x_out = call(
        functools.partial(y_sweep, sizes),
        [block] + [(16 + rows - early_rows(rows), lanes)] * len(x_rounds),
        partial, w_rims, opened, ay, cy, cx, *y_in,
        name="y_sweep", flops=10**10,
    )
    x_late = [swap(m, p) for m, p in zip(x_out, x_rounds)]
    ready = call(
        x_inner, [(4, rows, lanes)] + [(planes - 2, rows, lanes)] * 2, g, opened, ax, cx, name="x_inner"
    )
    (out,) = call(
        functools.partial(x_sweep, sizes), [block], g, ax, cx, *ready, *x_early, *x_late,
        target=pltpu.HBM, name="x_sweep",
        scratch=[pltpu.VMEM(block, jnp.float32), dma((planes,))],
    )
    return out


def solution(mesh):
    sizes = tuple(mesh.shape[axis] for axis in AXES)
    placed = P(*AXES)
    return jax.shard_map(
        functools.partial(per_device, sizes),
        mesh=mesh,
        in_specs=(placed,) * 8,
        out_specs=placed,
        check_vma=False,
    )
```

```python
import functools
import itertools

import jax
import jax.numpy as jnp
from jax import lax
from jax.experimental import pallas as pl
from jax.experimental.pallas import tpu as pltpu
from jax.sharding import PartitionSpec as P

sharpness = 3.5
slot = 8
AXES = ("gx", "gy", "gz")


def colours(sizes, along):
    return min(sizes[along] - 1, 3 if along == 2 else 2)


def turn_of(face, along, n):
    return (face + (1 if along == 0 else 0)) % n


def pair_rounds(sizes, along, aside=0):
    n = colours(sizes, along)

    def partner(at, turn):
        at = list(at)
        i = at[along]
        if turn_of(i, along, n) == turn and i + 1 < sizes[along]:
            at[along] += 1
        elif i > 0 and turn_of(i - 1, along, n) == turn:
            at[along] -= 1
        elif aside == along:
            at[along] = sizes[along] - 1 - i
        elif sizes[aside] % 2 == 0:
            at[aside] ^= 1
        return at

    places = list(itertools.product(*(range(size) for size in sizes)))
    flat = lambda at: (at[0] * sizes[1] + at[1]) * sizes[2] + at[2]
    return [[(flat(at), flat(partner(at, turn))) for at in places] for turn in range(n)]


def to_send(sizes, along, up, down):
    n, at = colours(sizes, along), lax.axis_index(AXES[along])
    if n <= 1:
        return [jnp.where(at == 0, up, down)] * n
    mine = turn_of(at, along, n)
    return [jnp.where((mine == turn) & (at < sizes[along] - 1), up, down) for turn in range(n)]


def received(sizes, along, messages, like):
    n, at = colours(sizes, along), lax.axis_index(AXES[along])
    if n == 0:
        return jnp.zeros_like(like), jnp.zeros_like(like)
    low = high = messages[0]
    for turn in range(1, n):
        low = jnp.where(turn_of(at + n - 1, along, n) == turn, messages[turn], low)
        high = jnp.where(turn_of(at, along, n) == turn, messages[turn], high)
    return jnp.where(at > 0, low, 0.0), jnp.where(at < sizes[along] - 1, high, 0.0)


def bend(a, difference):
    t = jnp.tanh(sharpness * difference)
    return t, 0.5 * sharpness * a * (1.0 - a) * (1.0 - t * t)


def low_end(low, w0, w1, a0, a1, c0):
    w_far, w_low, a_far, a_low, c_far, c_low = low
    _, bent = bend(a_low, a0 - a_far)
    across = w0 - w_low
    r_low = (across * jnp.maximum(c_low, 0.0) - (w_low - w_far) * jnp.minimum(c_far, 0.0)) * bent
    forth = (w1 - w0) * jnp.maximum(c0, 0.0)
    back = across * jnp.minimum(c_low, 0.0)
    t, bent = bend(a0, a1 - a_low)
    first = w0 * (c0 - c_low) + (forth + back) + (forth - back) * ((0.5 - a0) * t) + r_low
    return first, (forth - back) * bent


def high_end(high, w0, w1, a0, a1, c0, c1):
    w_high, w_far, a_high, a_far, c_high = high
    _, bent = bend(a_high, a_far - a1)
    across = w_high - w1
    r_high = ((w_far - w_high) * jnp.maximum(c_high, 0.0) - across * jnp.minimum(c1, 0.0)) * bent
    forth = across * jnp.maximum(c1, 0.0)
    back = (w1 - w0) * jnp.minimum(c0, 0.0)
    t, bent = bend(a1, a_high - a0)
    last = w1 * (c1 - c0) + (forth + back) + (forth - back) * ((0.5 - a1) * t) - r_high
    return last, (back - forth) * bent


def factors(a, c, dim):
    length = a.shape[dim]
    at = lax.broadcasted_iota(jnp.int32, a.shape, dim)
    inside = (at > 0) & (at < length - 1)
    below = pltpu.roll(c, 1, dim)
    t, bent = bend(a, pltpu.roll(a, length - 1, dim) - pltpu.roll(a, 1, dim))
    return (
        jnp.where(inside, c - below, 0.0),
        jnp.where(inside, jnp.maximum(c, 0.0), 0.0),
        jnp.where(inside, jnp.minimum(below, 0.0), 0.0),
        (0.5 - a) * t,
        bent,
    )


def interior(g, w, parts, dim):
    rise, ahead, behind, lean, bent = parts
    length = w.shape[dim]
    prev = lambda value: pltpu.roll(value, 1, dim)
    after = lambda value: pltpu.roll(value, length - 1, dim)
    forth = (after(w) - w) * ahead
    back = (w - prev(w)) * behind
    apart = forth - back
    r = apart * bent
    return g + (w * rise + (forth + back) + apart * lean) + (prev(r) - after(r))


def fold(planes, rows, lanes):
    per = lanes // (slot * planes)
    return per if per >= 1 and rows % (8 * per) == 0 else 1


def edge_lanes(shape, lanes):
    at = lax.broadcasted_iota(jnp.int32, shape, 1)
    return at, lax.rem(at, slot)


def z_pack(sizes, planes, rows, lanes, *refs):
    sources, targets, (w_ref, edge_ref, *out, sems) = refs[:4], refs[4:8], refs[8:]
    copies = [
        [
            pltpu.make_async_copy(src.at[x], dst.at[x], sems.at[n, x])
            for n, (src, dst) in enumerate(zip(sources, targets))
        ]
        for x in range(planes)
    ]
    for copy in itertools.chain(*copies):
        copy.start()
    cot, opened, a_ref, c_ref = targets
    per = fold(planes, rows, lanes)
    step = rows // per
    at, place = edge_lanes((rows, lanes), lanes)
    near = (at < 2) | (at >= lanes - 2)
    totals = [None] * 2
    for x in range(planes):
        for copy in itertools.chain(*({0: copies[:2], 2: copies[2:]}.get(x, []))):
            copy.wait()
        w = cot[x] * opened[x].astype(jnp.float32)
        w_ref[x] = w
        for n, field, lane in ((0, w, 2), (0, a_ref[x], 6), (1, c_ref[x], 4)):
            field = jnp.where(near, field, 0.0)
            for r in range(per):
                part = field[r * step : (r + 1) * step]
                part = pltpu.roll(part, (slot * (x + planes * r) + lane) % lanes, 1)
                totals[n] = part if totals[n] is None else totals[n] + part
    for n in range(2):
        edge_ref[n] = totals[n]
    _, place = edge_lanes((step, lanes), lanes)
    up = jnp.where(lax.rem(place, 4) < 2, totals[0], jnp.where(place < 4, totals[1], 0.0))
    down = jnp.where(lax.rem(place, 4) >= 2, totals[0], jnp.where(place >= 4, totals[1], 0.0))
    for ref, message in zip(out, to_send(sizes, 2, up, down)):
        ref[...] = message


def lane(value, at):
    lanes = value.shape[1]
    return pltpu.roll(value, lanes - at, 1) if at else value


def z_inner(g_ref, w_ref, a_ref, c_ref, edges, out, own):
    for x in range(a_ref.shape[0]):
        out[x] = interior(g_ref[x], w_ref[x], factors(a_ref[x], c_ref[x], 1), 1)
    for n, at in enumerate((2, 3, 6, 7, 0, 1, 4, 5)):
        own[n] = lane(edges[0], at)
    for n, at in enumerate((4, 2, 3)):
        own[8 + n] = lane(edges[1], at)


def y_base(planes):
    return (2 * planes + 7) // 8 * 8


def y_factors(sizes, ay, cy, *out):
    planes, rows, lanes = ay.shape
    for x in range(planes):
        for ref, part in zip(out, factors(ay[x], cy[x], 0)):
            ref[x] = part
        for n, field in enumerate((ay, cy)):
            at = y_base(planes) + 4 * x + 2 * n
            for ref, pair in zip(out[5:], to_send(sizes, 1, field[x, rows - 2 :], field[x, :2])):
                ref[at : at + 2] = pair


def z_ends(own, low, high):
    w_far, w_low, c_far, c_low, a_far, a_low = (lane(low, at) for at in range(6))
    first, second = low_end((w_far, w_low, a_far, a_low, c_far, c_low), *own[:4], own[8])
    w_high, w_far, c_high, a_high, a_far = (lane(high, at) for at in (2, 3, 4, 6, 7))
    last, before = high_end((w_high, w_far, a_high, a_far, c_high), *own[4:8], *own[9:])
    return first, second, last, before


columns = (0, 1, -1, -2)


def spread(ends, x, r, planes, lanes, column=0):
    move = (column - slot * (x + planes * r)) % lanes
    return pltpu.roll(ends, move, 1) if move else ends


def on_columns(at, lanes, values):
    total = 0.0
    for column, value in zip(columns, values):
        total = jnp.where(at == column % lanes, value, total)
    return total


def z_sweep(sizes, partial, own, opened, ax, cx, *rest):
    n_in, n_y = colours(sizes, 2), colours(sizes, 1)
    others, messages = rest[:n_y], [m[...] for m in rest[n_y : n_y + n_in]]
    ends_ref, *out = rest[n_y + n_in :]
    planes, rows, lanes = partial.shape
    per = fold(planes, rows, lanes)
    step = rows // per
    low, high = received(sizes, 2, messages, own[0])
    ends = z_ends([own[n] for n in range(11)], low, high)
    _, place = edge_lanes((step, lanes), lanes)
    ends_ref[...] = on_columns(
        place, slot, [spread(end, 0, 0, planes, lanes, column) for end, column in zip(ends, columns)]
    )
    if not out:
        return
    at = lax.broadcasted_iota(jnp.int32, (8, lanes), 1)
    for x in range(planes):
        ws = []
        for rim, group, r in ((slice(0, 8), slice(0, 8), 0), (slice(rows - 8, rows), slice(step - 8, step), per - 1)):
            added = [
                spread(end[group], x, r, planes, lanes, column) for end, column in zip(ends, columns)
            ]
            g = partial[x, rim] + on_columns(at, lanes, added)
            ws.append(opened[x, rim].astype(jnp.float32) * g)
        for ref, pair in zip(out, to_send(sizes, 1, ws[1][6:], ws[0][:2])):
            ref[2 * x : 2 * x + 2] = pair
    base = y_base(planes)
    for other, ref in zip(others, out):
        ref[base:] = other[base:]


def x_products(w, cx):
    planes = len(w)
    back = (w[-1] - w[-2]) * jnp.minimum(cx[planes - 2], 0.0)
    forth = (w[1] - w[0]) * jnp.maximum(cx[0], 0.0)
    return (w[-1], w[0]), (back, forth)


def early_rows(rows):
    return rows * 5 // 64 * 8


def y_inner(sizes, partial_z, ends_ref, opened, ax, cx, *rest):
    parts_y, (partial, w_rims, *out) = rest[:5], rest[5:]
    planes, rows, lanes = ax.shape
    ends = ends_ref[...]
    at = lax.broadcasted_iota(jnp.int32, (rows, lanes), 1)
    near = (at < 2) | (at >= lanes - 2)
    tile = lax.broadcasted_iota(jnp.int32, (8, lanes), 0)
    per = fold(planes, rows, lanes)
    ws = []
    for x in range(planes):
        mask = opened[x].astype(jnp.float32)
        parts = jnp.concatenate([spread(ends, x, r, planes, lanes) for r in range(per)], axis=0)
        g = partial_z[x] + jnp.where(near, parts, 0.0)
        w = mask * g
        w_rims[x] = jnp.where(tile < 4, w[:8], w[rows - 8 :])
        g = interior(g, w, [part[x] for part in parts_y], 0)
        partial[x] = g
        ws.append(mask * g)
    pairs = (
        *x_products(ws, cx),
        (ax[planes - 2], ax[0]),
        (ax[planes - 1], ax[1]),
    )
    for v, (up, down) in enumerate(pairs):
        for ref, message in zip(out, to_send(sizes, 0, up, down)):
            ref[v * rows : (v + 1) * rows] = message
    half = slice(0, early_rows(rows))
    for ref, message in zip(out, to_send(sizes, 0, cx[planes - 1, half], cx[0, half])):
        ref[4 * rows :] = message


def y_sweep(sizes, partial, w_rims, opened, ay, cy, cx, *rest):
    n_in = colours(sizes, 1)
    messages, (g_ref, *out) = rest[:n_in], rest[n_in:]
    planes, rows, lanes = ay.shape
    tile = lax.broadcasted_iota(jnp.int32, (8, lanes), 0)
    ws = []
    base = y_base(planes)
    all_low, all_high = received(sizes, 1, [m[...] for m in messages], ay[0, : base + 4 * planes])
    for x in range(planes):
        low, high = (
            [value[n : n + 1] for n in (2 * x, 2 * x + 1, *range(base + 4 * x, base + 4 * x + 4))]
            for value in (all_low, all_high)
        )
        row = lambda ref, n: ref[x, n : n + 1]
        first, second = low_end(
            low,
            *(row(ref, n) for ref, n in ((w_rims, 0), (w_rims, 1), (ay, 0), (ay, 1), (cy, 0))),
        )
        last, before = high_end(
            high[:5],
            row(w_rims, 6),
            row(w_rims, 7),
            *(row(ref, n) for ref in (ay, cy) for n in (rows - 2, rows - 1)),
        )
        top = partial[x, :8] + jnp.where(tile == 0, first, jnp.where(tile == 1, second, 0.0))
        bottom = partial[x, rows - 8 :] + jnp.where(
            tile == 7, last, jnp.where(tile == 6, before, 0.0)
        )
        g_ref[x, :8] = top
        g_ref[x, 8 : rows - 8] = partial[x, 8 : rows - 8]
        g_ref[x, rows - 8 :] = bottom
        mask = jnp.where(tile < 4, opened[x, :8], opened[x, rows - 8 :]).astype(jnp.float32)
        ws.append(mask * jnp.where(tile < 4, top, bottom))
    if out:
        c = [jnp.where(tile < 4, cx[x, :8], cx[x, rows - 8 :]) for x in range(planes)]
        for v, (up, down) in enumerate(x_products(ws, c)):
            for ref, message in zip(out, to_send(sizes, 0, up, down)):
                ref[8 * v : 8 * v + 8] = message
        half = slice(early_rows(rows), rows)
        for ref, message in zip(out, to_send(sizes, 0, cx[planes - 1, half], cx[0, half])):
            ref[16:] = message


def x_inner(g_ref, opened, ax, cx, ready, own_ref, r_ref):
    planes = ax.shape[0]
    last = planes - 1
    w = [opened[x].astype(jnp.float32) * g_ref[x] for x in range(planes)]
    ready[0], ready[1] = w[0], w[last]
    ready[2] = (w[1] - w[0]) * jnp.maximum(cx[0], 0.0)
    ready[3] = (w[last] - w[last - 1]) * jnp.minimum(cx[last - 1], 0.0)
    for x in range(1, last):
        t, bent = bend(ax[x], ax[x + 1] - ax[x - 1])
        forth = (w[x + 1] - w[x]) * jnp.maximum(cx[x], 0.0)
        back = (w[x] - w[x - 1]) * jnp.minimum(cx[x - 1], 0.0)
        apart = forth - back
        r_ref[x - 1] = apart * bent
        own_ref[x - 1] = (
            g_ref[x] + w[x] * (cx[x] - cx[x - 1]) + (forth + back) + apart * ((0.5 - ax[x]) * t)
        )


def x_sweep(sizes, g_ref, ax, cx, ready, own_ref, r_ref, *rest):
    n_in = colours(sizes, 0)
    early, late, (out, stage, sems) = rest[:n_in], rest[n_in : 2 * n_in], rest[2 * n_in :]
    planes, rows, lanes = ax.shape
    last = planes - 1
    tile = lax.broadcasted_iota(jnp.int32, (8, lanes), 0)

    def whole(n, v):
        if v == 4:
            return jnp.concatenate([early[n][4 * rows :], late[n][16:]], axis=0)
        value = early[n][v * rows : (v + 1) * rows]
        if v > 1:
            return value
        ends = late[n][8 * v : 8 * v + 8]
        top = jnp.where(tile < 2, ends, value[:8])
        bottom = jnp.where(tile >= 6, ends, value[rows - 8 :])
        return jnp.concatenate([top, value[8 : rows - 8], bottom], axis=0)

    (w_low, w_high), (b_low, f_high), (f0, h0), (f1, h1), (c_low, _) = (
        received(sizes, 0, [whole(n, v) for n in range(n_in)], ax[0]) for v in range(5)
    )
    copies = []

    def leave(x, value):
        stage[x] = value
        copies.append(pltpu.make_async_copy(stage.at[x], out.at[x], sems.at[x]))
        copies[-1].start()

    def outer(x, w, a_next, forth, back, c_low):
        t, bent = bend(ax[x], a_next)
        apart = forth - back
        own = g_ref[x] + w * (cx[x] - c_low) + (forth + back) + apart * ((0.5 - ax[x]) * t)
        return own, apart * bent

    w_first, w_last = ready[0], ready[1]
    across = w_first - w_low
    own_first, r_first = outer(
        0, w_first, ax[1] - f1, ready[2], across * jnp.minimum(c_low, 0.0), c_low
    )
    _, bent = bend(f1, ax[0] - f0)
    r_low = (across * jnp.maximum(c_low, 0.0) - b_low) * bent
    across = w_high - w_last
    own_last, r_last = outer(
        last, w_last, h0 - ax[last - 1], across * jnp.maximum(cx[last], 0.0), ready[3], cx[last - 1]
    )
    _, bent = bend(h0, h1 - ax[last])
    r_high = (f_high - across * jnp.minimum(cx[last], 0.0)) * bent
    r = [r_low, r_first, *(r_ref[x] for x in range(last - 1)), r_last, r_high]
    for x in range(planes):
        own = own_first if x == 0 else own_last if x == last else own_ref[x - 1]
        leave(x, own + (r[x] - r[x + 2]))
    for copy in copies:
        copy.wait()


def call(body, out, *args, name, loads=(), scratch=(), flops=0, target=pltpu.VMEM):
    shapes = [jax.ShapeDtypeStruct(o, jnp.float32) if isinstance(o, tuple) else o for o in out]
    loads = [pltpu.with_memory_space_constraint(v, pltpu.HBM) for v in loads]
    return pl.pallas_call(
        body,
        out_shape=shapes,
        in_specs=[pl.BlockSpec(memory_space=pltpu.VMEM)] * len(args)
        + [pl.BlockSpec(memory_space=pltpu.HBM)] * len(loads),
        out_specs=[pl.BlockSpec(memory_space=target)] * len(shapes),
        scratch_shapes=scratch,
        compiler_params=pltpu.CompilerParams(vmem_limit_bytes=8 * 2**20),
        cost_estimate=pl.CostEstimate(flops=flops, bytes_accessed=2**20, transcendentals=0),
        name=name,
    )(*args, *loads)


def per_device(sizes, cot, ax, ay, az, cx, cy, cz, opened):
    x_rounds, y_rounds, z_rounds = (pair_rounds(sizes, d) for d in range(3))
    early_rounds = pair_rounds(sizes, 0, 1)
    x_rounds = pair_rounds(sizes, 0, 0)
    block = az.shape
    planes, rows, lanes = block
    swap = lambda value, perm: lax.ppermute(value, AXES, perm)
    packed = (rows // fold(planes, rows, lanes), lanes)
    dma = pltpu.SemaphoreType.DMA
    cot, opened, az, cz, w, edges, *z_out = call(
        functools.partial(z_pack, sizes, planes, rows, lanes),
        [block, jax.ShapeDtypeStruct(block, jnp.int32), block, block, block, (2, *packed)]
        + [packed] * len(z_rounds),
        loads=(cot, opened, az, cz),
        name="z_pack", scratch=[dma((4, planes))],
    )
    z_in = [swap(m, p) for m, p in zip(z_out, z_rounds)]
    partial, own = call(z_inner, [block, (11, *packed)], cot, w, az, cz, edges, name="z_inner")
    factors_y = call(
        functools.partial(y_factors, sizes),
        [block] * 5 + [(y_base(planes) + 4 * planes, lanes)] * len(y_rounds),
        ay, cy,
        name="y_factors",
    )
    parts_y, others_y = factors_y[:5], factors_y[5:]
    ends, *y_out = call(
        functools.partial(z_sweep, sizes),
        [packed] + [(y_base(planes) + 4 * planes, lanes)] * len(y_rounds),
        partial, own, opened, ax, cx, *others_y, *z_in,
        name="z_sweep",
    )
    y_in = [swap(m, p) for m, p in zip(y_out, y_rounds)]
    partial, w_rims, *x_out = call(
        functools.partial(y_inner, sizes),
        [block, (planes, 8, lanes)] + [(4 * rows + early_rows(rows), lanes)] * len(x_rounds),
        partial, ends, opened, ax, cx, *parts_y,
        name="y_inner",
    )
    x_early = [swap(m, p) for m, p in zip(x_out, early_rounds)]
    g, *x_out = call(
        functools.partial(y_sweep, sizes),
        [block] + [(16 + rows - early_rows(rows), lanes)] * len(x_rounds),
        partial, w_rims, opened, ay, cy, cx, *y_in,
        name="y_sweep", flops=10**10,
    )
    x_late = [swap(m, p) for m, p in zip(x_out, x_rounds)]
    ready = call(
        x_inner, [(4, rows, lanes)] + [(planes - 2, rows, lanes)] * 2, g, opened, ax, cx, name="x_inner"
    )
    (out,) = call(
        functools.partial(x_sweep, sizes), [block], g, ax, cx, *ready, *x_early, *x_late,
        target=pltpu.HBM, name="x_sweep",
        scratch=[pltpu.VMEM(block, jnp.float32), dma((planes,))],
    )
    return out


def solution(mesh):
    sizes = tuple(mesh.shape[axis] for axis in AXES)
    placed = P(*AXES)
    return jax.shard_map(
        functools.partial(per_device, sizes),
        mesh=mesh,
        in_specs=(placed,) * 8,
        out_specs=placed,
        check_vma=False,
    )
```

```python
import functools
import itertools

import jax
import jax.numpy as jnp
from jax import lax
from jax.experimental import pallas as pl
from jax.experimental.pallas import tpu as pltpu
from jax.sharding import PartitionSpec as P

sharpness = 3.5
slot = 8
AXES = ("gx", "gy", "gz")


def colours(sizes, along):
    return min(sizes[along] - 1, 3 if along == 2 else 2)


def turn_of(face, along, n):
    return (face + (1 if along == 0 else 0)) % n


def pair_rounds(sizes, along, aside=0):
    n = colours(sizes, along)

    def partner(at, turn):
        at = list(at)
        i = at[along]
        if turn_of(i, along, n) == turn and i + 1 < sizes[along]:
            at[along] += 1
        elif i > 0 and turn_of(i - 1, along, n) == turn:
            at[along] -= 1
        elif aside == along:
            at[along] = sizes[along] - 1 - i
        elif sizes[aside] % 2 == 0:
            at[aside] ^= 1
        return at

    places = list(itertools.product(*(range(size) for size in sizes)))
    flat = lambda at: (at[0] * sizes[1] + at[1]) * sizes[2] + at[2]
    return [[(flat(at), flat(partner(at, turn))) for at in places] for turn in range(n)]


def to_send(sizes, along, up, down):
    n, at = colours(sizes, along), lax.axis_index(AXES[along])
    if n <= 1:
        return [jnp.where(at == 0, up, down)] * n
    mine = turn_of(at, along, n)
    return [jnp.where((mine == turn) & (at < sizes[along] - 1), up, down) for turn in range(n)]


def received(sizes, along, messages, like):
    n, at = colours(sizes, along), lax.axis_index(AXES[along])
    if n == 0:
        return jnp.zeros_like(like), jnp.zeros_like(like)
    low = high = messages[0]
    for turn in range(1, n):
        low = jnp.where(turn_of(at + n - 1, along, n) == turn, messages[turn], low)
        high = jnp.where(turn_of(at, along, n) == turn, messages[turn], high)
    return jnp.where(at > 0, low, 0.0), jnp.where(at < sizes[along] - 1, high, 0.0)


def bend(a, difference):
    t = jnp.tanh(sharpness * difference)
    return t, 0.5 * sharpness * a * (1.0 - a) * (1.0 - t * t)


def low_end(low, w0, w1, a0, a1, c0):
    w_far, w_low, a_far, a_low, c_far, c_low = low
    _, bent = bend(a_low, a0 - a_far)
    across = w0 - w_low
    r_low = (across * jnp.maximum(c_low, 0.0) - (w_low - w_far) * jnp.minimum(c_far, 0.0)) * bent
    forth = (w1 - w0) * jnp.maximum(c0, 0.0)
    back = across * jnp.minimum(c_low, 0.0)
    t, bent = bend(a0, a1 - a_low)
    first = w0 * (c0 - c_low) + (forth + back) + (forth - back) * ((0.5 - a0) * t) + r_low
    return first, (forth - back) * bent


def high_end(high, w0, w1, a0, a1, c0, c1):
    w_high, w_far, a_high, a_far, c_high = high
    _, bent = bend(a_high, a_far - a1)
    across = w_high - w1
    r_high = ((w_far - w_high) * jnp.maximum(c_high, 0.0) - across * jnp.minimum(c1, 0.0)) * bent
    forth = across * jnp.maximum(c1, 0.0)
    back = (w1 - w0) * jnp.minimum(c0, 0.0)
    t, bent = bend(a1, a_high - a0)
    last = w1 * (c1 - c0) + (forth + back) + (forth - back) * ((0.5 - a1) * t) - r_high
    return last, (back - forth) * bent


def factors(a, c, dim):
    length = a.shape[dim]
    at = lax.broadcasted_iota(jnp.int32, a.shape, dim)
    inside = (at > 0) & (at < length - 1)
    below = pltpu.roll(c, 1, dim)
    t, bent = bend(a, pltpu.roll(a, length - 1, dim) - pltpu.roll(a, 1, dim))
    return (
        jnp.where(inside, c - below, 0.0),
        jnp.where(inside, jnp.maximum(c, 0.0), 0.0),
        jnp.where(inside, jnp.minimum(below, 0.0), 0.0),
        (0.5 - a) * t,
        bent,
    )


def interior(g, w, parts, dim):
    rise, ahead, behind, lean, bent = parts
    length = w.shape[dim]
    prev = lambda value: pltpu.roll(value, 1, dim)
    after = lambda value: pltpu.roll(value, length - 1, dim)
    forth = (after(w) - w) * ahead
    back = (w - prev(w)) * behind
    apart = forth - back
    r = apart * bent
    return g + (w * rise + (forth + back) + apart * lean) + (prev(r) - after(r))


def fold(planes, rows, lanes):
    per = lanes // (slot * planes)
    return per if per >= 1 and rows % (8 * per) == 0 else 1


def edge_lanes(shape, lanes):
    at = lax.broadcasted_iota(jnp.int32, shape, 1)
    return at, lax.rem(at, slot)


def z_pack(sizes, planes, rows, lanes, *refs):
    sources, targets, (w_ref, edge_ref, *out, sems) = refs[:4], refs[4:8], refs[8:]
    copies = [
        [
            pltpu.make_async_copy(src.at[x], dst.at[x], sems.at[n, x])
            for n, (src, dst) in enumerate(zip(sources, targets))
        ]
        for x in range(planes)
    ]
    for copy in itertools.chain(*copies):
        copy.start()
    cot, opened, a_ref, c_ref = targets
    per = fold(planes, rows, lanes)
    step = rows // per
    at, place = edge_lanes((rows, lanes), lanes)
    near = (at < 2) | (at >= lanes - 2)
    totals = [None] * 2
    for x in range(planes):
        for copy in itertools.chain(*({0: copies[:2], 2: copies[2:]}.get(x, []))):
            copy.wait()
        w = cot[x] * opened[x].astype(jnp.float32)
        w_ref[x] = w
        for n, field, lane in ((0, w, 2), (0, a_ref[x], 6), (1, c_ref[x], 4)):
            field = jnp.where(near, field, 0.0)
            for r in range(per):
                part = field[r * step : (r + 1) * step]
                part = pltpu.roll(part, (slot * (x + planes * r) + lane) % lanes, 1)
                totals[n] = part if totals[n] is None else totals[n] + part
    for n in range(2):
        edge_ref[n] = totals[n]
    _, place = edge_lanes((step, lanes), lanes)
    up = jnp.where(lax.rem(place, 4) < 2, totals[0], jnp.where(place < 4, totals[1], 0.0))
    down = jnp.where(lax.rem(place, 4) >= 2, totals[0], jnp.where(place >= 4, totals[1], 0.0))
    for ref, message in zip(out, to_send(sizes, 2, up, down)):
        ref[...] = message


def z_inner(g_ref, w_ref, a_ref, c_ref, ay_in, cy_in, out, ay, cy, *rest):
    parts, sems = rest[:5], rest[5]
    copies = [
        pltpu.make_async_copy(src, dst, sems.at[n])
        for n, (src, dst) in enumerate(((ay_in, ay), (cy_in, cy)))
    ]
    for copy in copies:
        copy.start()
    planes = a_ref.shape[0]
    for x in range(planes):
        out[x] = interior(g_ref[x], w_ref[x], factors(a_ref[x], c_ref[x], 1), 1)
    for copy in copies:
        copy.wait()
    for x in range(planes):
        for ref, part in zip(parts, factors(ay[x], cy[x], 0)):
            ref[x] = part


def z_ends(edges, low, high, lanes):
    lane = lambda value, at: pltpu.roll(value, lanes - at, 1) if at else value
    wa, c = edges
    w_far, w_low, c_far, c_low, a_far, a_low = (lane(low, at) for at in range(6))
    first, second = low_end(
        (w_far, w_low, a_far, a_low, c_far, c_low),
        *(lane(wa, at) for at in (2, 3, 6, 7)),
        lane(c, 4),
    )
    w_high, w_far, c_high, a_high, a_far = (lane(high, at) for at in (2, 3, 4, 6, 7))
    last, before = high_end(
        (w_high, w_far, a_high, a_far, c_high),
        *(lane(wa, at) for at in (0, 1, 4, 5)),
        *(lane(c, at) for at in (2, 3)),
    )
    return first, second, last, before


columns = (0, 1, -1, -2)


def spread(ends, x, r, planes, lanes, column=0):
    move = (column - slot * (x + planes * r)) % lanes
    return pltpu.roll(ends, move, 1) if move else ends


def on_columns(at, lanes, values):
    total = 0.0
    for column, value in zip(columns, values):
        total = jnp.where(at == column % lanes, value, total)
    return total


def z_sweep(sizes, partial, edges, opened, ay, cy, ax, cx, *rest):
    n_in = colours(sizes, 2)
    messages, (ends_ref, *out) = [m[...] for m in rest[:n_in]], rest[n_in:]
    planes, rows, lanes = ay.shape
    per = fold(planes, rows, lanes)
    step = rows // per
    low, high = received(sizes, 2, messages, edges[0])
    ends = z_ends([edges[0], edges[1]], low, high, lanes)
    _, place = edge_lanes((step, lanes), lanes)
    ends_ref[...] = on_columns(
        place, slot, [spread(end, 0, 0, planes, lanes, column) for end, column in zip(ends, columns)]
    )
    if not out:
        return
    at = lax.broadcasted_iota(jnp.int32, (8, lanes), 1)
    tile = lax.broadcasted_iota(jnp.int32, (8, lanes), 0)
    for x in range(planes):
        ws = []
        for rim, group, r in ((slice(0, 8), slice(0, 8), 0), (slice(rows - 8, rows), slice(step - 8, step), per - 1)):
            added = [
                spread(end[group], x, r, planes, lanes, column) for end, column in zip(ends, columns)
            ]
            g = partial[x, rim] + on_columns(at, lanes, added)
            ws.append(opened[x, rim].astype(jnp.float32) * g)
        a, c = (pltpu.roll(ref[x, rows - 8 :], by, 0) for ref, by in ((ay, 6), (cy, 4)))
        up = jnp.where(tile >= 6, ws[1], jnp.where(tile >= 4, a, c))
        a, c = (pltpu.roll(ref[x, :8], by, 0) for ref, by in ((ay, 2), (cy, 4)))
        down = jnp.where(tile < 2, ws[0], jnp.where(tile < 4, a, c))
        for ref, message in zip(out, to_send(sizes, 1, up, down)):
            ref[x] = message


def x_products(w, cx):
    planes = len(w)
    back = (w[-1] - w[-2]) * jnp.minimum(cx[planes - 2], 0.0)
    forth = (w[1] - w[0]) * jnp.maximum(cx[0], 0.0)
    return (w[-1], w[0]), (back, forth)


def early_rows(rows):
    return rows * 5 // 64 * 8


def y_inner(sizes, partial_z, ends_ref, opened, ax, cx, *rest):
    parts_y, (partial, w_rims, *out) = rest[:5], rest[5:]
    planes, rows, lanes = ax.shape
    ends = ends_ref[...]
    at = lax.broadcasted_iota(jnp.int32, (rows, lanes), 1)
    near = (at < 2) | (at >= lanes - 2)
    tile = lax.broadcasted_iota(jnp.int32, (8, lanes), 0)
    per = fold(planes, rows, lanes)
    ws = []
    for x in range(planes):
        mask = opened[x].astype(jnp.float32)
        parts = jnp.concatenate([spread(ends, x, r, planes, lanes) for r in range(per)], axis=0)
        g = partial_z[x] + jnp.where(near, parts, 0.0)
        w = mask * g
        w_rims[x] = jnp.where(tile < 4, w[:8], w[rows - 8 :])
        g = interior(g, w, [part[x] for part in parts_y], 0)
        partial[x] = g
        ws.append(mask * g)
    pairs = (
        *x_products(ws, cx),
        (ax[planes - 2], ax[0]),
        (ax[planes - 1], ax[1]),
    )
    for v, (up, down) in enumerate(pairs):
        for ref, message in zip(out, to_send(sizes, 0, up, down)):
            ref[v * rows : (v + 1) * rows] = message
    half = slice(0, early_rows(rows))
    for ref, message in zip(out, to_send(sizes, 0, cx[planes - 1, half], cx[0, half])):
        ref[4 * rows :] = message


def y_sweep(sizes, partial, w_rims, opened, ay, cy, cx, *rest):
    n_in = colours(sizes, 1)
    messages, (g_ref, *out) = rest[:n_in], rest[n_in:]
    planes, rows, lanes = ay.shape
    tile = lax.broadcasted_iota(jnp.int32, (8, lanes), 0)
    ws = []
    for x in range(planes):
        low, high = received(sizes, 1, [m[x] for m in messages], ay[x, :8])
        row = lambda ref, n: ref[x, n : n + 1]
        first, second = low_end(
            [low[v : v + 1] for v in (6, 7, 4, 5, 2, 3)],
            *(row(ref, n) for ref, n in ((w_rims, 0), (w_rims, 1), (ay, 0), (ay, 1), (cy, 0))),
        )
        last, before = high_end(
            [high[v : v + 1] for v in range(5)],
            row(w_rims, 6),
            row(w_rims, 7),
            *(row(ref, n) for ref in (ay, cy) for n in (rows - 2, rows - 1)),
        )
        top = partial[x, :8] + jnp.where(tile == 0, first, jnp.where(tile == 1, second, 0.0))
        bottom = partial[x, rows - 8 :] + jnp.where(
            tile == 7, last, jnp.where(tile == 6, before, 0.0)
        )
        g_ref[x, :8] = top
        g_ref[x, 8 : rows - 8] = partial[x, 8 : rows - 8]
        g_ref[x, rows - 8 :] = bottom
        mask = jnp.where(tile < 4, opened[x, :8], opened[x, rows - 8 :]).astype(jnp.float32)
        ws.append(mask * jnp.where(tile < 4, top, bottom))
    if out:
        c = [jnp.where(tile < 4, cx[x, :8], cx[x, rows - 8 :]) for x in range(planes)]
        for v, (up, down) in enumerate(x_products(ws, c)):
            for ref, message in zip(out, to_send(sizes, 0, up, down)):
                ref[8 * v : 8 * v + 8] = message
        half = slice(early_rows(rows), rows)
        for ref, message in zip(out, to_send(sizes, 0, cx[planes - 1, half], cx[0, half])):
            ref[16:] = message


def x_inner(g_ref, opened, ax, cx, ready, own_ref, r_ref):
    planes = ax.shape[0]
    last = planes - 1
    w = [opened[x].astype(jnp.float32) * g_ref[x] for x in range(planes)]
    ready[0], ready[1] = w[0], w[last]
    ready[2] = (w[1] - w[0]) * jnp.maximum(cx[0], 0.0)
    ready[3] = (w[last] - w[last - 1]) * jnp.minimum(cx[last - 1], 0.0)
    for x in range(1, last):
        t, bent = bend(ax[x], ax[x + 1] - ax[x - 1])
        forth = (w[x + 1] - w[x]) * jnp.maximum(cx[x], 0.0)
        back = (w[x] - w[x - 1]) * jnp.minimum(cx[x - 1], 0.0)
        apart = forth - back
        r_ref[x - 1] = apart * bent
        own_ref[x - 1] = (
            g_ref[x] + w[x] * (cx[x] - cx[x - 1]) + (forth + back) + apart * ((0.5 - ax[x]) * t)
        )


def x_sweep(sizes, g_ref, ax, cx, ready, own_ref, r_ref, *rest):
    n_in = colours(sizes, 0)
    early, late, (out, stage, sems) = rest[:n_in], rest[n_in : 2 * n_in], rest[2 * n_in :]
    planes, rows, lanes = ax.shape
    last = planes - 1
    tile = lax.broadcasted_iota(jnp.int32, (8, lanes), 0)

    def whole(n, v):
        if v == 4:
            return jnp.concatenate([early[n][4 * rows :], late[n][16:]], axis=0)
        value = early[n][v * rows : (v + 1) * rows]
        if v > 1:
            return value
        ends = late[n][8 * v : 8 * v + 8]
        top = jnp.where(tile < 2, ends, value[:8])
        bottom = jnp.where(tile >= 6, ends, value[rows - 8 :])
        return jnp.concatenate([top, value[8 : rows - 8], bottom], axis=0)

    (w_low, w_high), (b_low, f_high), (f0, h0), (f1, h1), (c_low, _) = (
        received(sizes, 0, [whole(n, v) for n in range(n_in)], ax[0]) for v in range(5)
    )
    copies = []

    def leave(x, value):
        stage[x] = value
        copies.append(pltpu.make_async_copy(stage.at[x], out.at[x], sems.at[x]))
        copies[-1].start()

    def outer(x, w, a_next, forth, back, c_low):
        t, bent = bend(ax[x], a_next)
        apart = forth - back
        own = g_ref[x] + w * (cx[x] - c_low) + (forth + back) + apart * ((0.5 - ax[x]) * t)
        return own, apart * bent

    w_first, w_last = ready[0], ready[1]
    across = w_first - w_low
    own_first, r_first = outer(
        0, w_first, ax[1] - f1, ready[2], across * jnp.minimum(c_low, 0.0), c_low
    )
    _, bent = bend(f1, ax[0] - f0)
    r_low = (across * jnp.maximum(c_low, 0.0) - b_low) * bent
    across = w_high - w_last
    own_last, r_last = outer(
        last, w_last, h0 - ax[last - 1], across * jnp.maximum(cx[last], 0.0), ready[3], cx[last - 1]
    )
    _, bent = bend(h0, h1 - ax[last])
    r_high = (f_high - across * jnp.minimum(cx[last], 0.0)) * bent
    r = [r_low, r_first, *(r_ref[x] for x in range(last - 1)), r_last, r_high]
    for x in range(planes):
        own = own_first if x == 0 else own_last if x == last else own_ref[x - 1]
        leave(x, own + (r[x] - r[x + 2]))
    for copy in copies:
        copy.wait()


def call(body, out, *args, name, loads=(), scratch=(), flops=0, target=pltpu.VMEM):
    shapes = [jax.ShapeDtypeStruct(o, jnp.float32) if isinstance(o, tuple) else o for o in out]
    loads = [pltpu.with_memory_space_constraint(v, pltpu.HBM) for v in loads]
    return pl.pallas_call(
        body,
        out_shape=shapes,
        in_specs=[pl.BlockSpec(memory_space=pltpu.VMEM)] * len(args)
        + [pl.BlockSpec(memory_space=pltpu.HBM)] * len(loads),
        out_specs=[pl.BlockSpec(memory_space=target)] * len(shapes),
        scratch_shapes=scratch,
        compiler_params=pltpu.CompilerParams(vmem_limit_bytes=8 * 2**20),
        cost_estimate=pl.CostEstimate(flops=flops, bytes_accessed=2**20, transcendentals=0),
        name=name,
    )(*args, *loads)


def per_device(sizes, cot, ax, ay, az, cx, cy, cz, opened):
    x_rounds, y_rounds, z_rounds = (pair_rounds(sizes, d) for d in range(3))
    early_rounds = pair_rounds(sizes, 0, 1)
    x_rounds = pair_rounds(sizes, 0, 0)
    block = az.shape
    planes, rows, lanes = block
    swap = lambda value, perm: lax.ppermute(value, AXES, perm)
    packed = (rows // fold(planes, rows, lanes), lanes)
    dma = pltpu.SemaphoreType.DMA
    cot, opened, az, cz, w, edges, *z_out = call(
        functools.partial(z_pack, sizes, planes, rows, lanes),
        [block, jax.ShapeDtypeStruct(block, jnp.int32), block, block, block, (2, *packed)]
        + [packed] * len(z_rounds),
        loads=(cot, opened, az, cz),
        name="z_pack", scratch=[dma((4, planes))],
    )
    z_in = [swap(m, p) for m, p in zip(z_out, z_rounds)]
    partial, ay, cy, *parts_y = call(
        z_inner, [block] * 8, cot, w, az, cz, loads=(ay, cy), name="z_inner", scratch=[dma((2,))]
    )
    ends, *y_out = call(
        functools.partial(z_sweep, sizes),
        [packed] + [(planes, 8, lanes)] * len(y_rounds),
        partial, edges, opened, ay, cy, ax, cx, *z_in,
        name="z_sweep",
    )
    y_in = [swap(m, p) for m, p in zip(y_out, y_rounds)]
    partial, w_rims, *x_out = call(
        functools.partial(y_inner, sizes),
        [block, (planes, 8, lanes)] + [(4 * rows + early_rows(rows), lanes)] * len(x_rounds),
        partial, ends, opened, ax, cx, *parts_y,
        name="y_inner",
    )
    x_early = [swap(m, p) for m, p in zip(x_out, early_rounds)]
    g, *x_out = call(
        functools.partial(y_sweep, sizes),
        [block] + [(16 + rows - early_rows(rows), lanes)] * len(x_rounds),
        partial, w_rims, opened, ay, cy, cx, *y_in,
        name="y_sweep", flops=10**10,
    )
    x_late = [swap(m, p) for m, p in zip(x_out, x_rounds)]
    ready = call(
        x_inner, [(4, rows, lanes)] + [(planes - 2, rows, lanes)] * 2, g, opened, ax, cx, name="x_inner"
    )
    (out,) = call(
        functools.partial(x_sweep, sizes), [block], g, ax, cx, *ready, *x_early, *x_late,
        target=pltpu.HBM, name="x_sweep",
        scratch=[pltpu.VMEM(block, jnp.float32), dma((planes,))],
    )
    return out


def solution(mesh):
    sizes = tuple(mesh.shape[axis] for axis in AXES)
    placed = P(*AXES)
    return jax.shard_map(
        functools.partial(per_device, sizes),
        mesh=mesh,
        in_specs=(placed,) * 8,
        out_specs=placed,
        check_vma=False,
    )
```
